32 devices in a mesh: shard: 8 (over z, x), replica: 4 (over y, core).
Axes of the slice: x: 2, y: 2, z: 4, core: 2. Of those that a mesh axis runs over, the one named last changes fastest.
Arguments:
- tokens: bfloat16 [128, 197, 512], P(('shard', 'replica')), may hold values from -6 to 6
- routes: int32 [128, 197, 2], P(('shard', 'replica')), may hold values from 0 to 7, all different within a row; in each aligned block of 788 rows (0 to 787, 788 to 1575, ..., all dimensions but the last counted through in order) at most 376 rows name the same one
- live_images: int32 [32], P(('shard', 'replica')), may hold values from 3 to 4, as said below
- cotangent: bfloat16 [128, 197, 512], P(('shard', 'replica')), may hold values from -6 to 6
- norm_one_gain: bfloat16 [512], P('shard'), may hold values from 0.5 to 1.5
- norm_one_bias: bfloat16 [512], P('shard'), may hold values from -1.75 to 1.75
- qkv_weight: bfloat16 [512, 1536], P('shard'), may hold values from -0.25 to 0.25
- query_value_bias: bfloat16 [2, 512], P(None, 'shard'), may hold values from -1.75 to 1.75
- output_weight: bfloat16 [512, 512], P('shard'), may hold values from -2 to 2
- output_bias: bfloat16 [512], P('shard'), may hold values from -1.75 to 1.75
- norm_two_gain: bfloat16 [512], P('shard'), may hold values from 0.5 to 1.5
- norm_two_bias: bfloat16 [512], P('shard'), may hold values from -1.75 to 1.75
- router_weight: bfloat16 [512, 8], P('shard'), may hold values from -0.1875 to 0.1875
- expert_up: bfloat16 [8, 512, 2048], P(None, None, 'shard'), may hold values from -0.25 to 0.25
- expert_up_bias: bfloat16 [8, 2048], P(None, 'shard'), may hold values from -1.75 to 1.75
- expert_down: bfloat16 [8, 2048, 512], P(None, 'shard'), may hold values from -0.5 to 0.5
- expert_down_bias: bfloat16 [8, 512], P(None, 'shard'), may hold values from -1.75 to 1.75
Outputs:
- mixed: bfloat16 [128, 197, 512], P(('shard', 'replica'))
- grad_tokens: bfloat16 [128, 197, 512], P(('shard', 'replica'))
- grad_norm_one_gain: float32 [512], P('shard')
- grad_norm_one_bias: float32 [512], P('shard')
- grad_qkv_weight: float32 [512, 1536], P('shard')
- grad_query_value_bias: float32 [2, 512], P(None, 'shard')
- grad_output_weight: float32 [512, 512], P('shard')
- grad_output_bias: float32 [512], P('shard')
- grad_norm_two_gain: float32 [512], P('shard')
- grad_norm_two_bias: float32 [512], P('shard')
- grad_router_weight: float32 [512, 8], P('shard')
- grad_expert_up: float32 [8, 512, 2048], P(None, None, 'shard')
- grad_expert_up_bias: float32 [8, 2048], P(None, 'shard')
- grad_expert_down: float32 [8, 2048, 512], P(None, 'shard')
- grad_expert_down_bias: float32 [8, 512], P(None, 'shard')
The draws below stay inside these ranges and needn't reach their ends.
Inputs may be any that keep to these rules, and one draw needn't show every extreme that they name: `routes`: the two experts of a token differ. Among the 788 tokens of one device no expert is named more than 376 times, a bound that some block reaches. `live_images`: each device has 3 or 4 live images; both values occur in every draw.
All inputs are finite; a program needn't handle non-finite values.
Results may differ from the reference program's by a relative error of at most 0.02.
Values may be sent and summed in bfloat16 or wider, within the bound.
No kernel may reach another device: no remote copies, remote signals or barrier semaphores. Data moves between devices by JAX's collectives and lax.ppermute only.
A program may use at most 320 MiB of HBM per device.

```python
import math
import jax
import jax.numpy as jnp
import numpy as np
from jax import lax

D = 512
HEADS = 8
FF = 2048
LEN = 197
EXPERTS = 8
TOP = 2
IMG_DEV = 4
CAP = 376
IMAGES = 128
DEVICES = 32


def draw_live_images(key, part):
    key = jax.random.fold_in(key, 7)
    first_key, second_key, third_key = jax.random.split(key, 3)
    lowest = max(1, IMG_DEV - 1)
    coin_flip = jax.random.randint(first_key, (DEVICES,), 0, 4)
    counts = jnp.where(coin_flip == 0, lowest, IMG_DEV).astype(jnp.int32)
    full_spot = jax.random.randint(second_key, (), 0, DEVICES)
    short_spot = (full_spot + 1 + jax.random.randint(third_key, (), 0, DEVICES - 1)) % DEVICES
    counts = counts.at[full_spot].set(IMG_DEV).at[short_spot].set(lowest)
    return counts.astype(jnp.int32)


def steps_of(key, extent, pieces, least, top_value):
    factor_of = 1.0
    for dim, parts in pieces:
        heights = jax.random.uniform(jax.random.fold_in(jax.random.fold_in(key, 6), dim), (parts,), jnp.float32, least / len(pieces), top_value / len(pieces))
        factor_of = factor_of * jnp.repeat(jnp.exp(heights), extent[dim] // parts).reshape((-1,) + (1,) * (len(extent) - 1 - dim))
    return factor_of


def routed_block(rng, own, number, rows, amount, top, most, lean):
    sequence = jax.random.permutation(rng, amount)
    heavy_load, usual = load_shares(amount, rows * top, most, lean, True), load_shares(amount, rows * top, most, lean, False)
    places = jnp.arange(amount)

    def named(sizes, turn):
        used = int((sizes > 0).sum())
        fixed = max(1, used // 4)
        shifted = fixed + (places - fixed + turn * (used - fixed)) % max(1, amount - fixed)
        return jnp.zeros((amount,), jnp.int32).at[sequence[jnp.where(places < fixed, places, shifted)]].set(jnp.asarray(sizes, jnp.int32))

    sizes = jnp.where(number % 4 == 0, named(heavy_load, number // 4), named(usual, number - number // 4 - 1))
    mixed = jax.random.permutation(jax.random.fold_in(own, 3), amount)
    giver, receiver = mixed[0:amount // 2 * 2:2], mixed[1:amount // 2 * 2:2]
    slack = jnp.minimum(sizes[giver] - 1, most - sizes[receiver]) // 2
    slack = jnp.where((giver == sequence[0]) | (receiver == sequence[0]) | (sizes[receiver] == 0), 0, jnp.maximum(slack, 0))
    shifted = jax.random.randint(jax.random.fold_in(own, 4), (amount // 2,), 0, 1 << 20) % (slack + 1)
    sizes = sizes.at[giver].add(-shifted).at[receiver].add(shifted)
    labels = jnp.searchsorted(jnp.cumsum(sizes), jnp.arange(rows * top), side="right").astype(jnp.int32)
    table = labels.reshape(top, rows).T
    table = table[jax.random.permutation(jax.random.fold_in(own, 1), rows)]
    turn = jax.random.randint(jax.random.fold_in(own, 2), (rows, 1), 0, top)
    return jnp.take_along_axis(table, (jnp.arange(top)[None, :] + turn) % top, axis=1)


def load_shares(number_of, total, reach, slope, full):
    loads = [(1 << 20) // math.isqrt(standing ** slope) + 1 for standing in range(1, number_of + 1)]
    largest = reach if full else min(reach, max(-(-total // number_of), total * loads[0] // sum(loads)))
    least = 1 if total - largest >= number_of - 1 else 0
    given, rest = [largest] + [least] * (number_of - 1), total - largest - least * (number_of - 1)
    while rest > 0:
        candidates = [i for i in range(1, number_of) if given[i] < largest] or [i for i in range(1, number_of) if given[i] < reach]
        whole, left = sum([loads[i] for i in candidates]), rest
        for i in candidates:
            more = min(reach - given[i], max(1, left * loads[i] // whole), rest)
            given[i] = given[i] + more
            rest = rest - more
    return np.array(given)


def bell_draw(key, dims, spread, bound, pieces=(), kind=jnp.bfloat16):
    loudness = steps_of(key, dims, pieces, -0.22, 0.18) if pieces else 1.0
    array = jax.random.normal(key, dims, jnp.float32) * spread * loudness
    return jnp.minimum(jnp.maximum(array, -bound), bound).astype(kind)


def setup_inputs(seed: int = 0) -> dict:
    key_list = jax.random.split(jax.random.key(seed), 18)
    tokens = bell_draw(key_list[0], (IMAGES, LEN, D), 1.0, 6.0, ((0, 32),))
    routes_keys = jax.random.split(jax.random.fold_in(key_list[1], 1), IMAGES * LEN // (IMG_DEV * LEN))
    routes_turns = jax.random.permutation(jax.random.fold_in(key_list[1], 3), IMAGES * LEN // (IMG_DEV * LEN))
    routes = jax.vmap(lambda own, number: routed_block(jax.random.fold_in(key_list[1], 2), own, number, IMG_DEV * LEN, EXPERTS, TOP, CAP, 1))(routes_keys, routes_turns).reshape((IMAGES, LEN, TOP))
    live_images = draw_live_images(jax.random.fold_in(key_list[17], 71), 0)
    cotangent = bell_draw(key_list[3], (IMAGES, LEN, D), 1.0, 6.0, ((0, 32),))
    norm_one_gain = jnp.clip(1.0 + 0.1 * jax.random.normal(key_list[4], (D,), jnp.float32), 0.5, 1.5).astype(jnp.bfloat16)
    norm_one_bias = bell_draw(key_list[5], (D,), 0.3, 1.75, ((0, 8),))
    qkv_weight = bell_draw(key_list[6], (D, 3 * D), D ** -0.5, 0.25, ((0, 8),))
    query_value_bias = bell_draw(key_list[7], (2, D), 0.3, 1.75, ((1, 8),))
    output_weight = bell_draw(key_list[8], (D, D), (D // 64) ** -0.5, 2.0, ((0, 8),))
    output_bias = bell_draw(key_list[9], (D,), 0.3, 1.75, ((0, 8),))
    norm_two_gain = jnp.clip(1.0 + 0.1 * jax.random.normal(key_list[10], (D,), jnp.float32), 0.5, 1.5).astype(jnp.bfloat16)
    norm_two_bias = bell_draw(key_list[11], (D,), 0.3, 1.75, ((0, 8),))
    router_weight = bell_draw(key_list[12], (D, EXPERTS), 0.033, 0.1875, ((0, 8),))
    expert_up = bell_draw(key_list[13], (EXPERTS, D, FF), D ** -0.5, 0.25, ((2, 8),))
    expert_up_bias = bell_draw(key_list[14], (EXPERTS, FF), 0.3, 1.75, ((1, 8),))
    expert_down = bell_draw(key_list[15], (EXPERTS, FF, D), (FF // 16) ** -0.5, 0.5, ((1, 8),))
    expert_down_bias = bell_draw(key_list[16], (EXPERTS, D), 0.3, 1.75, ((1, 8),))
    return dict(tokens=tokens, routes=routes, live_images=live_images, cotangent=cotangent, norm_one_gain=norm_one_gain, norm_one_bias=norm_one_bias, qkv_weight=qkv_weight, query_value_bias=query_value_bias, output_weight=output_weight, output_bias=output_bias, norm_two_gain=norm_two_gain, norm_two_bias=norm_two_bias, router_weight=router_weight, expert_up=expert_up, expert_up_bias=expert_up_bias, expert_down=expert_down, expert_down_bias=expert_down_bias)


@jax.custom_vjp
def low(v):
    return lax.optimization_barrier(v.astype(jnp.bfloat16)).astype(jnp.float32)

@jax.custom_vjp
def low_back(v):
    return v

def low_keep(v):
    return (low(v), None)

def low_pass(kept, grad):
    return (grad,)

def back_keep(v):
    return (v, None)

def back_low(kept, grad):
    return (low(grad),)
low.defvjp(low_keep, low_pass)
low_back.defvjp(back_keep, back_low)
NORM_EPS = 1e-06
highest = lax.Precision.HIGHEST

def layer_norm(values, gain_vec, bias_vec):
    center_mean = lax.optimization_barrier(jnp.mean(values, -1, keepdims=True))
    centered = values - center_mean
    variance = lax.optimization_barrier(jnp.mean(centered * centered, -1, keepdims=True))
    return centered * lax.rsqrt(variance + NORM_EPS) * gain_vec + bias_vec

def both_ways(values):
    return low(low_back(values))

def dispatch_slots(route_flat):
    row_count = route_flat.shape[0] // TOP
    one_hot = (route_flat[:, None] == jnp.arange(EXPERTS, dtype=jnp.int32)[None, :]).astype(jnp.int32)
    before = jnp.cumsum(one_hot, axis=0) - one_hot
    position = lax.optimization_barrier(jnp.sum(before * one_hot, axis=1))
    slot_ids = (route_flat * CAP + position).astype(jnp.int32)
    owners = jnp.repeat(jnp.arange(row_count, dtype=jnp.int32), TOP)
    slot_table = jnp.full((EXPERTS * CAP,), row_count, jnp.int32).at[slot_ids].set(owners)
    return (slot_ids, slot_table)

def block_forward(block_tokens, block_routes, block_keep, params):
    norm_one_gain, norm_one_bias, qkv_weight, query_value_bias, output_weight, output_bias, norm_two_gain, norm_two_bias, router_weight, expert_up, expert_up_bias, expert_down, expert_down_bias = params
    images_here, seq_len, model_width = block_tokens.shape
    row_count = images_here * seq_len
    head_size = model_width // HEADS
    scale_factor = head_size ** (-0.5)
    first_in = low(layer_norm(block_tokens, norm_one_gain, norm_one_bias)).reshape(row_count, model_width)
    projected = jnp.dot(first_in, qkv_weight, precision=highest).reshape(images_here, seq_len, 3, HEADS, head_size)
    queries = both_ways(projected[:, :, 0] + query_value_bias[0].reshape(HEADS, head_size))
    keys_all = both_ways(projected[:, :, 1])
    values_all = both_ways(projected[:, :, 2] + query_value_bias[1].reshape(HEADS, head_size))
    scores = low_back(jnp.einsum('ilhd,imhd->ihlm', queries, keys_all, precision=highest) * scale_factor)
    soft_low = low(jax.nn.softmax(scores, axis=-1))
    attended = both_ways(jnp.einsum('ihlm,imhd->ilhd', soft_low, values_all, precision=highest).reshape(row_count, model_width))
    branch = low_back(jnp.dot(attended, output_weight, precision=highest) + output_bias)
    middle = block_tokens.reshape(row_count, model_width) + branch
    hidden_in = low(layer_norm(middle, norm_two_gain, norm_two_bias))
    logits = jnp.dot(hidden_in, router_weight, precision=highest)
    router_probs = jax.nn.softmax(logits, axis=-1)
    route_rows = block_routes.reshape(row_count, TOP)
    gate_values = jnp.take_along_axis(router_probs, route_rows, axis=1)
    slot_ids, slot_table = dispatch_slots(route_rows.reshape(-1))
    padded = jnp.concatenate([hidden_in, jnp.zeros((1, model_width), jnp.float32)], axis=0)
    expert_rows = padded[slot_table].reshape(EXPERTS, CAP, model_width)
    pre_act = low_back(jnp.einsum('ecd,edf->ecf', expert_rows, expert_up, precision=highest) + expert_up_bias[:, None, :])
    active_low = low(jax.nn.gelu(pre_act, approximate=False))
    expert_result = low_back(jnp.einsum('ecf,efd->ecd', active_low, expert_down, precision=highest) + expert_down_bias[:, None, :])
    picked = expert_result.reshape(EXPERTS * CAP, model_width)[slot_ids].reshape(row_count, TOP, model_width)
    mixture = lax.optimization_barrier(jnp.sum(gate_values[:, :, None] * picked, axis=1))
    row_keep = jnp.repeat(block_keep, seq_len)[:, None]
    return ((middle + mixture) * row_keep).reshape(images_here, seq_len, model_width)

def reference(tokens, routes, live_images, cotangent, norm_one_gain, norm_one_bias, qkv_weight, query_value_bias, output_weight, output_bias, norm_two_gain, norm_two_bias, router_weight, expert_up, expert_up_bias, expert_down, expert_down_bias):
    weight_list = (norm_one_gain, norm_one_bias, qkv_weight, query_value_bias, output_weight, output_bias, norm_two_gain, norm_two_bias, router_weight, expert_up, expert_up_bias, expert_down, expert_down_bias)
    params = tuple((weight_item.astype(jnp.float32) for weight_item in weight_list))
    start_tokens = tokens.astype(jnp.float32).reshape(DEVICES, IMG_DEV, LEN, D)
    block_routes = routes.reshape(DEVICES, IMG_DEV, LEN, TOP)
    keep_mask = (jnp.arange(IMG_DEV, dtype=jnp.int32)[None, :] < live_images[:, None]).astype(jnp.float32)

    def forward(token_blocks, param_set):

        def one_block(packed):
            return block_forward(packed[0], packed[1], packed[2], param_set)
        return lax.map(jax.checkpoint(one_block), (token_blocks, block_routes, keep_mask))
    outputs, pullback = jax.vjp(forward, start_tokens, params)
    grad_start, grad_params = pullback(cotangent.astype(jnp.float32).reshape(start_tokens.shape))
    return (outputs.reshape(IMAGES, LEN, D).astype(jnp.bfloat16), grad_start.reshape(IMAGES, LEN, D).astype(jnp.bfloat16), grad_params[0], grad_params[1], grad_params[2], grad_params[3], grad_params[4], grad_params[5], grad_params[6], grad_params[7], grad_params[8], grad_params[9], grad_params[10], grad_params[11], grad_params[12])
```

```python
import functools
import math

import jax
import jax.numpy as jnp
from jax import lax
from jax.experimental import pallas as pl
from jax.experimental.pallas import tpu as pltpu
from jax.sharding import PartitionSpec as P

HEADS = 8
EXPERTS = 8
TOP = 2
NORM_EPS = 1e-06
TILE = 256
SEG = 16
LANES = 128
BF = jnp.bfloat16
F32 = jnp.float32


def layer_norm(values, gain_vec, bias_vec):
    center_mean = jnp.mean(values, -1, keepdims=True)
    centered = values - center_mean
    variance = jnp.mean(centered * centered, -1, keepdims=True)
    return centered * lax.rsqrt(variance + NORM_EPS) * gain_vec + bias_vec


def cycle_order(count):
    if count % 2 or count < 4:
        return list(range(count))
    return list(range(0, count, 2)) + list(range(count - 1, 0, -2))


class Links:
    def __init__(self, shards, copies):
        self.shards, self.copies = shards, copies
        self.team = min(4, copies)
        self.order = cycle_order(shards)
        self.place = [self.order.index(s) for s in range(shards)]
        ring = self.order + self.order[:1]
        self.ahead = [(ring[i], ring[i + 1]) for i in range(shards)]
        self.back = [(b, a) for a, b in self.ahead]
        self.team_bits = [1 << i for i in range(self.team.bit_length() - 1)]
        self.other_bits = []
        bit = self.team
        while bit < copies:
            self.other_bits.append(bit)
            bit *= 2

    def ring_ahead(self, value):
        return lax.ppermute(value, "shard", self.ahead)

    def ring_back(self, value):
        return lax.ppermute(value, "shard", self.back)

    def swap(self, value, bit):
        return lax.ppermute(value, "replica", [(i, i ^ bit) for i in range(self.copies)])

    def my_place(self):
        return jnp.asarray(self.place, jnp.int32)[lax.axis_index("shard")]

    def my_copy(self):
        return lax.axis_index("replica")


def add_low(first, second):
    return (first.astype(F32) + second.astype(F32)).astype(BF)


def expert_kernel(images, experts, chunks, team, meta, *refs):
    hid, cot, posr, posc = refs[:4]
    ups = refs[4 : 4 + chunks]
    downs = refs[4 + chunks : 4 + 2 * chunks]
    ub, db, router = refs[4 + 2 * chunks : 7 + 2 * chunks]
    mix, dhid, gup, gdn, gub, grt, gdb = refs[7 + 2 * chunks : 14 + 2 * chunks]
    xb, tb, ax, xt, tt, at, wu, wd, gu_acc, gd_acc, gb_acc = refs[14 + 2 * chunks :]
    step = pl.program_id(0)
    slots = xt.shape[0]
    tokens = hid.shape[1]
    width = hid.shape[2]
    table = images * experts

    def dot(a, b):
        return lax.dot_general(a, b, (((1,), (0,)), ((), ())), preferred_element_type=F32)

    def dot_nt(a, b):
        return lax.dot_general(a, b, (((1,), (1,)), ((), ())), preferred_element_type=F32)

    def dot_tn(a, b):
        return lax.dot_general(a, b, (((0,), (0,)), ((), ())), preferred_element_type=F32)

    def probabilities(h):
        logits = dot(h, router[...])
        lane = lax.broadcasted_iota(jnp.int32, logits.shape, 1)
        logits = jnp.where(lane < experts, logits, -1e30)
        top = jnp.max(logits, axis=1, keepdims=True)
        e = jnp.exp(logits - top)
        return e / jnp.sum(e, axis=1, keepdims=True)

    @pl.when(step == 0)
    def _():
        grt[...] = jnp.zeros_like(grt)
        gdb[...] = jnp.zeros_like(gdb)
        xt[...] = jnp.zeros_like(xt)
        tt[...] = jnp.zeros_like(tt)
        at[...] = jnp.zeros_like(at)

    @pl.when(step < images)
    def _():
        h = hid[0]
        c = cot[0]
        row = lax.broadcasted_iota(jnp.int32, (slots, tokens), 0)
        pick = (row == posr[0, 0:1, :]) | (row == posr[0, 1:2, :])
        pick = jnp.where(pick, 1.0, 0.0).astype(BF)
        probs = probabilities(h)
        high = probs.astype(BF)
        low = (probs - high.astype(F32)).astype(BF)
        xt[...] = dot(pick, h).astype(BF)
        tt[...] = dot(pick, c).astype(BF)
        at[...] = dot(pick, high) + dot(pick, low)
        for e in range(experts):
            where = step * experts + e
            src = meta[where]
            dst = meta[table + where]

            def copy(k, carry, src=src, dst=dst):
                s = pl.multiple_of(src + k * SEG, SEG)
                d = pl.multiple_of(dst + k * SEG, SEG)
                xb[pl.ds(d, SEG), :] = xt[pl.ds(s, SEG), :]
                tb[pl.ds(d, SEG), :] = tt[pl.ds(s, SEG), :]
                ax[pl.ds(d, SEG), :] = at[pl.ds(s, SEG), :]
                return carry

            lax.fori_loop(0, meta[2 * table + where], copy, 0)

    @pl.when((step >= images) & (step < images + experts))
    def _():
        e = step - images
        start = meta[3 * table + e]
        tiles = meta[3 * table + experts + e]
        used = meta[3 * table + 2 * experts + e]
        part = ups[0].shape[1]
        for k in range(chunks):
            wu[k * part : (k + 1) * part, :] = ups[k][0]
            wd[k * part : (k + 1) * part, :] = downs[k][0]

        def clear(k, carry):
            d = pl.multiple_of(start + used + k * SEG, SEG)
            xb[pl.ds(d, SEG), :] = jnp.zeros((SEG, width), BF)
            tb[pl.ds(d, SEG), :] = jnp.zeros((SEG, width), BF)
            ax[pl.ds(d, SEG), :] = jnp.zeros((SEG, LANES), F32)
            return carry

        lax.fori_loop(0, (tiles * TILE - used) // SEG, clear, 0)
        gu_acc[...] = jnp.zeros_like(gu_acc)
        gd_acc[...] = jnp.zeros_like(gd_acc)
        gb_acc[...] = jnp.zeros_like(gb_acc)

        def tile(j, carry):
            at_row = pl.multiple_of(start + j * TILE, SEG)
            here = pl.ds(at_row, TILE)
            x = xb[here, :]
            t = tb[here, :]
            extra = ax[here, :]
            lane = lax.broadcasted_iota(jnp.int32, extra.shape, 1)
            gate = jnp.sum(jnp.where(lane == e, extra, 0.0), axis=1, keepdims=True)
            pre = dot_nt(x, wu[...]) + ub[0]
            u = 1.0 / (1.0 + (0.3275911 * math.sqrt(0.5)) * jnp.abs(pre))
            bell = jnp.exp(-0.5 * pre * pre)
            poly = 1.421413741 + u * (-1.453152027 + u * 1.061405429)
            poly = u * (0.254829592 + u * (-0.284496736 + u * poly))
            half = (0.5 * poly) * bell
            phi = jnp.where(pre >= 0, 1.0 - half, half)
            active = (pre * phi).astype(BF)
            active_float = active.astype(F32)
            slope = phi + pre * bell * (1.0 / math.sqrt(2.0 * math.pi))
            raw = dot_nt(t, wd[...])
            score = jnp.sum(active_float * raw, axis=1, keepdims=True)
            gated = (gate * active_float).astype(BF)
            dpre = ((gate * raw) * slope).astype(BF)
            gd_acc[...] += dot_tn(gated, t)
            gu_acc[...] += dot_tn(dpre, x)
            gb_acc[...] += dot(jnp.ones((8, TILE), BF), dpre)
            xb[here, :] = dot(gated, wd[...]).astype(BF)
            tb[here, :] = dot(dpre, wu[...]).astype(BF)
            ax[here, :] = jnp.where(lane == e, score, 0.0)
            return carry

        lax.fori_loop(0, tiles, tile, 0)
        for k in range(chunks):
            gup[k, 0] = gu_acc[k * part : (k + 1) * part, :].astype(BF)
            gdn[k, 0] = gd_acc[k * part : (k + 1) * part, :].astype(BF)
        gub[0] = gb_acc[0:1, :]

    @pl.when(step >= images + experts)
    def _():
        image = step - images - experts
        for e in range(experts):
            where = image * experts + e
            dst = meta[where]
            src = meta[table + where]

            def copy(k, carry, src=src, dst=dst):
                s = pl.multiple_of(src + k * SEG, SEG)
                d = pl.multiple_of(dst + k * SEG, SEG)
                xt[pl.ds(d, SEG), :] = xb[pl.ds(s, SEG), :]
                tt[pl.ds(d, SEG), :] = tb[pl.ds(s, SEG), :]
                at[pl.ds(d, SEG), :] = ax[pl.ds(s, SEG), :]
                return carry

            lax.fori_loop(0, meta[2 * table + where], copy, 0)
        h = hid[0]
        c = cot[0]
        probs = probabilities(h)
        lane = lax.broadcasted_iota(jnp.int32, probs.shape, 1)
        routed = (lane == posc[0, :, 2:3]) | (lane == posc[0, :, 3:4])
        gates = (jnp.where(routed, probs, 0.0) * (1.0 / team)).astype(BF)
        slot = lax.broadcasted_iota(jnp.int32, (tokens, slots), 1)
        back = (slot == posc[0, :, 0:1]) | (slot == posc[0, :, 1:2])
        back = jnp.where(back, 1.0, 0.0).astype(BF)
        high = at[...].astype(BF)
        low = (at[...] - high.astype(F32)).astype(BF)
        mix[0] = (dot(back, xt[...]) + dot(gates, db[...])).astype(BF)
        dprobs = dot(back, high) + dot(back, low)
        dprobs = dprobs + jnp.where(routed, dot_nt(c, db[...]) * (1.0 / team), 0.0)
        dlogits = probs * (dprobs - jnp.sum(dprobs * probs, axis=1, keepdims=True))
        dlogits = dlogits.astype(BF)
        dhid[0] = (dot(back, tt[...]) + dot_nt(dlogits, router[...])).astype(BF)
        grt[...] += dot_tn(dlogits, h)
        gdb[...] += dot_tn(gates, c)


def expert_call(hid, cot, routes, ups, downs, up_bias, down_bias, router, team):
    images, tokens, width = hid.shape
    experts, part, _ = ups[0].shape
    chunks = len(ups)
    hidden = part * chunks
    pairs = TOP * tokens
    slots = (pairs + (SEG - 1) * experts) // SEG * SEG
    rows = images * slots + experts * TILE
    rows = (rows + TILE - 1) // TILE * TILE

    choice = (routes[..., None] == jnp.arange(experts, dtype=jnp.int32)).astype(F32)
    hot = jnp.sum(choice, axis=2)
    before = jnp.tril(jnp.ones((tokens, tokens), BF), -1)
    rank = jnp.einsum("ts,ise->ite", before, hot.astype(BF), preferred_element_type=F32)
    count = jnp.sum(hot, axis=1).astype(jnp.int32)
    groups = (count + SEG - 1) // SEG
    padded = groups * SEG
    local_start = jnp.cumsum(padded, axis=1) - padded
    used = jnp.sum(padded, axis=0)
    tiles = (used + TILE - 1) // TILE
    start = (jnp.cumsum(tiles) - tiles) * TILE
    global_start = start[None, :] + jnp.cumsum(padded, axis=0) - padded
    spot = rank + local_start[:, None, :].astype(F32)
    pos = jnp.sum(choice * spot[:, :, None, :], axis=3).astype(jnp.int32)
    posr = jnp.swapaxes(pos, 1, 2)
    posc = jnp.concatenate([pos, routes], axis=2)
    meta = jnp.concatenate(
        [
            local_start.reshape(-1),
            global_start.reshape(-1),
            groups.reshape(-1),
            start,
            tiles,
            used,
        ]
    ).astype(jnp.int32)

    def first(s, m):
        return jnp.where(s < images, s, jnp.clip(s - images - experts, 0, images - 1))

    def middle(s, m):
        return jnp.clip(s - images, 0, experts - 1)

    def last(s, m):
        return jnp.clip(s - images - experts, 0, images - 1)

    weight = pl.BlockSpec((1, part, width), lambda s, m: (middle(s, m), 0, 0))
    token = pl.BlockSpec((1, tokens, width), lambda s, m: (first(s, m), 0, 0))
    whole = lambda shape: pl.BlockSpec(shape, lambda s, m: (0,) * len(shape))
    grid_spec = pltpu.PrefetchScalarGridSpec(
        num_scalar_prefetch=1,
        grid=(2 * images + experts,),
        in_specs=[
            token,
            token,
            pl.BlockSpec((1, TOP, tokens), lambda s, m: (first(s, m), 0, 0)),
            pl.BlockSpec((1, tokens, 2 * TOP), lambda s, m: (first(s, m), 0, 0)),
            *[weight] * (2 * chunks),
            pl.BlockSpec((1, 1, hidden), lambda s, m: (middle(s, m), 0, 0)),
            whole((LANES, width)),
            whole((width, LANES)),
        ],
        out_specs=[
            pl.BlockSpec((1, tokens, width), lambda s, m: (last(s, m), 0, 0)),
            pl.BlockSpec((1, tokens, width), lambda s, m: (last(s, m), 0, 0)),
            pl.BlockSpec((chunks, 1, part, width), lambda s, m: (0, middle(s, m), 0, 0)),
            pl.BlockSpec((chunks, 1, part, width), lambda s, m: (0, middle(s, m), 0, 0)),
            pl.BlockSpec((1, 1, hidden), lambda s, m: (middle(s, m), 0, 0)),
            whole((LANES, width)),
            whole((LANES, width)),
        ],
        scratch_shapes=[
            pltpu.VMEM((rows, width), BF),
            pltpu.VMEM((rows, width), BF),
            pltpu.VMEM((rows, LANES), F32),
            pltpu.VMEM((slots, width), BF),
            pltpu.VMEM((slots, width), BF),
            pltpu.VMEM((slots, LANES), F32),
            pltpu.VMEM((hidden, width), BF),
            pltpu.VMEM((hidden, width), BF),
            pltpu.VMEM((hidden, width), F32),
            pltpu.VMEM((hidden, width), F32),
            pltpu.VMEM((8, hidden), F32),
        ],
    )
    pairs_all = images * pairs
    return pl.pallas_call(
        functools.partial(expert_kernel, images, experts, chunks, team),
        grid_spec=grid_spec,
        out_shape=[
            jax.ShapeDtypeStruct((images, tokens, width), BF),
            jax.ShapeDtypeStruct((images, tokens, width), BF),
            jax.ShapeDtypeStruct((chunks, experts, part, width), BF),
            jax.ShapeDtypeStruct((chunks, experts, part, width), BF),
            jax.ShapeDtypeStruct((experts, 1, hidden), F32),
            jax.ShapeDtypeStruct((LANES, width), F32),
            jax.ShapeDtypeStruct((LANES, width), F32),
        ],
        compiler_params=pltpu.CompilerParams(
            dimension_semantics=("arbitrary",), vmem_limit_bytes=60 * 1024 * 1024
        ),
        cost_estimate=pl.CostEstimate(
            flops=12 * pairs_all * hidden * width + 16 * images * slots * tokens * width,
            bytes_accessed=8 * images * tokens * width + 8 * experts * hidden * width,
            transcendentals=pairs_all * hidden,
        ),
        name="experts",
    )(meta, hid, cot, posr, posc, *ups, *downs, up_bias, down_bias, router)


def gather_team(links, value):
    for bit in reversed(links.team_bits):
        value = jnp.concatenate([value, links.swap(value, bit)], axis=0)
    return value


def reduce_team(links, value):
    for bit in links.team_bits:
        half = value.shape[0] // 2
        value = add_low(value[:half], links.swap(value[half:], bit))
    return value


def gather_quarters(links, value):
    value = value[None]
    for bit in reversed(links.team_bits):
        other = links.swap(value, bit)
        mine_low = (links.my_copy() & bit) == 0
        first = jnp.where(mine_low, value, other)
        second = jnp.where(mine_low, other, value)
        value = jnp.concatenate([first, second], axis=0)
    count = len(links.team_bits)
    shape = value.shape
    value = value.reshape((2,) * count + shape[1:])
    value = jnp.transpose(value, tuple(reversed(range(count))) + tuple(range(count, value.ndim)))
    return value.reshape(shape)


def ring_gather(links, value):
    blocks = [None] * links.shards
    blocks[0] = value
    forward = backward = value
    for j in range(1, links.shards // 2 + 1):
        forward = links.ring_ahead(forward)
        blocks[j] = forward
        if links.shards - j > j:
            backward = links.ring_back(backward)
            blocks[links.shards - j] = backward
    return blocks


def in_shard_order(links, blocks):
    count = links.shards
    stack = jnp.stack(blocks[::-1])
    start = jnp.mod(-links.my_place() - 1, count)
    ring = lax.dynamic_slice_in_dim(jnp.concatenate([stack, stack]), start, count, axis=0)
    return jnp.stack([ring[links.place[s]] for s in range(count)])


def from_shard_order(links, value):
    count = links.shards
    ring = jnp.stack([value[s] for s in links.order])
    return lax.dynamic_slice_in_dim(jnp.concatenate([ring, ring]), links.my_place(), count, axis=0)


def ring_reduce(links, value):
    count = links.shards
    half = count // 2
    total = value[0].astype(F32)
    part = value[half]
    for m in range(half - 1, -1, -1):
        part = links.ring_ahead(part)
        if m:
            part = add_low(part, value[m])
    total = total + part.astype(F32)
    if count > 2:
        part = value[half + 1]
        for m in range(half + 2, count + 1):
            part = links.ring_back(part)
            if m < count:
                part = add_low(part, value[m])
        total = total + part.astype(F32)
    return total


def reduce_dense(links, value):
    shards, team = links.shards, links.team
    rows = value.shape[0] // shards
    value = value.reshape(shards, rows, value.shape[1])
    for bit in links.team_bits:
        half = value.shape[1] // 2
        upper = (links.my_copy() & bit) != 0
        keep = jnp.where(upper, value[:, half:], value[:, :half])
        give = jnp.where(upper, value[:, :half], value[:, half:])
        value = add_low(keep, links.swap(give, bit))
    total = ring_reduce(links, from_shard_order(links, value))
    for bit in links.other_bits:
        total = total + links.swap(total, bit)
    value = total.astype(BF)
    for bit in reversed(links.team_bits):
        other = links.swap(value, bit)
        upper = (links.my_copy() & bit) != 0
        value = jnp.concatenate(
            [jnp.where(upper, other, value), jnp.where(upper, value, other)], axis=0
        )
    return value.astype(F32)


def local(
    links,
    tokens,
    routes,
    live_images,
    cotangent,
    norm_one_gain,
    norm_one_bias,
    qkv_weight,
    query_value_bias,
    output_weight,
    output_bias,
    norm_two_gain,
    norm_two_bias,
    router_weight,
    expert_up,
    expert_up_bias,
    expert_down,
    expert_down_bias,
):
    shards, team = links.shards, links.team
    images_here, seq_len, width = tokens.shape
    row_count = images_here * seq_len
    head_size = width // HEADS
    scale_factor = head_size ** (-0.5)
    d_rows = qkv_weight.shape[0]
    ff_rows = expert_down.shape[1]
    part = ff_rows // team
    member = links.my_copy() % team
    place = links.my_place()

    bias_columns = EXPERTS * ff_rows // d_rows
    columns = [
        router_weight,
        query_value_bias.T,
        norm_one_gain[:, None],
        norm_one_bias[:, None],
        norm_two_gain[:, None],
        norm_two_bias[:, None],
        output_bias[:, None],
        expert_down_bias.T,
        expert_up_bias.reshape(d_rows, bias_columns),
    ]
    sizes = [c.shape[1] for c in columns]
    pad = -sum(sizes) % LANES
    small = jnp.concatenate(columns + [jnp.zeros((d_rows, pad), BF)], axis=1)
    packed = jnp.concatenate([qkv_weight, output_weight, small], axis=1)
    if team > 1:
        half_rows = d_rows // 2
        core = member % 2
        mine = lax.dynamic_slice_in_dim(packed, core * half_rows, half_rows, axis=0)
        full = jnp.stack(ring_gather(links, mine))
        other = links.swap(full, 1)
        low = jnp.where(core == 0, full, other)
        high = jnp.where(core == 0, other, full)
        blocks = jnp.concatenate([low, high], axis=1)
    else:
        blocks = jnp.stack(ring_gather(links, packed))
    full = in_shard_order(links, [blocks[j] for j in range(shards)])
    full = full.reshape(width, packed.shape[1])
    qkv_full = full[:, : 3 * width]
    out_full = full[:, 3 * width : 4 * width]
    offsets = [4 * width]
    for size in sizes:
        offsets.append(offsets[-1] + size)
    cut = [full[:, offsets[i] : offsets[i + 1]] for i in range(len(sizes))]
    router_full = cut[0]
    qv_float = cut[1].astype(F32).T
    gain_one, bias_one, gain_two, bias_two, out_bias = (
        cut[i][:, 0].astype(F32) for i in range(2, 7)
    )
    down_bias_full = cut[7].T
    up_bias_shards = cut[8].reshape(shards, EXPERTS, ff_rows)

    up_part = lax.dynamic_slice_in_dim(expert_up, member * part, part, axis=2)
    up_part = jnp.swapaxes(up_part, 1, 2)
    down_part = lax.dynamic_slice_in_dim(expert_down, member * part, part, axis=1)
    up_part, down_part, blocks = lax.optimization_barrier((up_part, down_part, blocks))
    ups, downs = [up_part], [down_part]
    for _ in range(shards - 1):
        ups.append(links.ring_ahead(ups[-1]))
        downs.append(links.ring_back(downs[-1]))
    downs = [downs[-j % shards] for j in range(shards)]

    keep_images = (jnp.arange(images_here, dtype=jnp.int32) < live_images[0]).astype(F32)
    row_keep = jnp.repeat(keep_images, seq_len)[:, None]
    kept = cotangent * keep_images[:, None, None].astype(BF)
    cot_team = gather_team(links, kept)
    routes_team = gather_team(links, jnp.swapaxes(routes, 1, 2))
    routes_team = jnp.swapaxes(routes_team, 1, 2)

    float_tokens = tokens.astype(F32)
    normed_one, norm_one_back = jax.vjp(layer_norm, float_tokens, gain_one, bias_one)
    first_in = normed_one.astype(BF).reshape(row_count, width)
    projected = jnp.dot(first_in, qkv_full, preferred_element_type=F32)
    projected = projected.reshape(images_here, seq_len, 3, HEADS, head_size)
    queries = (projected[:, :, 0] + qv_float[0].reshape(HEADS, head_size)).astype(BF)
    keys_all = projected[:, :, 1].astype(BF)
    values_all = (projected[:, :, 2] + qv_float[1].reshape(HEADS, head_size)).astype(BF)

    def attention_scores():
        return (
            jnp.einsum("ilhd,imhd->ihlm", queries, keys_all, preferred_element_type=F32)
            * scale_factor
        )

    scores = attention_scores()
    score_top = jnp.max(scores, axis=-1, keepdims=True)
    log_total = score_top + jnp.log(jnp.sum(jnp.exp(scores - score_top), axis=-1, keepdims=True))
    soft_low = jnp.exp(scores - log_total).astype(BF)
    attended = jnp.einsum("ihlm,imhd->ilhd", soft_low, values_all, preferred_element_type=F32)
    attended = attended.reshape(row_count, width).astype(BF)
    branch = jnp.dot(attended, out_full, preferred_element_type=F32) + out_bias
    middle = float_tokens.reshape(row_count, width) + branch
    normed_two, norm_two_back = jax.vjp(layer_norm, middle, gain_two, bias_two)
    hidden_in = normed_two.astype(BF)

    hid_team = gather_team(links, hidden_in.reshape(images_here, seq_len, width))
    up_bias_mine = lax.dynamic_slice_in_dim(up_bias_shards, member * part, part, axis=2)
    up_bias_ahead = from_shard_order(links, up_bias_mine)
    up_bias_rel = jnp.stack([up_bias_ahead[-j % shards] for j in range(shards)])
    up_bias_rel = jnp.swapaxes(up_bias_rel, 0, 1).reshape(EXPERTS, 1, shards * part).astype(F32)
    down_bias_pad = jnp.pad(down_bias_full, ((0, LANES - EXPERTS), (0, 0)))
    router_pad = jnp.pad(router_full, ((0, 0), (0, LANES - EXPERTS)))
    mix_team, dhid_team, gup, gdn, gub, grt, gdb = expert_call(
        hid_team,
        cot_team,
        routes_team,
        ups,
        downs,
        up_bias_rel,
        down_bias_pad,
        router_pad,
        team,
    )

    part_up = gup[shards - 1]
    part_down = gdn[1 % shards]
    for j in range(shards - 2, -1, -1):
        part_up = add_low(links.ring_back(part_up), gup[j])
        part_down = add_low(links.ring_ahead(part_down), gdn[-j % shards])
    for bit in links.other_bits:
        part_up = add_low(part_up, links.swap(part_up, bit))
        part_down = add_low(part_down, links.swap(part_down, bit))

    dhidden = reduce_team(links, dhid_team).astype(F32).reshape(row_count, width)
    mixture = reduce_team(links, mix_team).astype(F32).reshape(row_count, width)
    mixed = ((middle + mixture) * row_keep).astype(BF).reshape(images_here, seq_len, width)

    dtotal = kept.astype(F32).reshape(row_count, width)
    dmiddle_norm, grad_gain_two, grad_bias_two = norm_two_back(dhidden)
    dmiddle = dtotal + dmiddle_norm
    dbranch = dmiddle.astype(BF)
    grad_out_bias = jnp.sum(dbranch, axis=0, dtype=F32)
    grad_out = jnp.dot(attended.T, dbranch, preferred_element_type=F32)
    dattended = jnp.dot(dbranch, out_full.T, preferred_element_type=F32)
    dattended = dattended.astype(BF).reshape(images_here, seq_len, HEADS, head_size)
    soft_again = jnp.exp(attention_scores() - log_total)
    dvalues = jnp.einsum(
        "ihlm,ilhd->imhd", soft_again.astype(BF), dattended, preferred_element_type=F32
    )
    dsoft = jnp.einsum("ilhd,imhd->ihlm", dattended, values_all, preferred_element_type=F32)
    dscores = soft_again * (dsoft - jnp.sum(dsoft * soft_again, axis=-1, keepdims=True))
    dscores = dscores.astype(BF)
    dqueries = (
        jnp.einsum("ihlm,imhd->ilhd", dscores, keys_all, preferred_element_type=F32) * scale_factor
    )
    dkeys = (
        jnp.einsum("ihlm,ilhd->imhd", dscores, queries, preferred_element_type=F32) * scale_factor
    )
    dprojected = jnp.stack([dqueries, dkeys, dvalues], axis=2).astype(BF)
    dprojected = dprojected.reshape(row_count, 3 * width)
    grad_qv = jnp.stack(
        [
            jnp.sum(dprojected[:, :width], axis=0, dtype=F32),
            jnp.sum(dprojected[:, 2 * width :], axis=0, dtype=F32),
        ]
    )
    grad_qkv = jnp.dot(first_in.T, dprojected, preferred_element_type=F32)
    dfirst = jnp.dot(dprojected, qkv_full.T, preferred_element_type=F32)
    dinput_norm, grad_gain_one, grad_bias_one = norm_one_back(
        dfirst.reshape(images_here, seq_len, width)
    )
    grad_tokens = (dmiddle.reshape(images_here, seq_len, width) + dinput_norm).astype(BF)

    gub_rel = jnp.swapaxes(gub.reshape(EXPERTS, shards, part), 0, 1)
    gub_shards = in_shard_order(links, [gub_rel[j] for j in range(shards)])
    gub_full = lax.dynamic_update_slice_in_dim(
        jnp.zeros((shards, EXPERTS, ff_rows), F32), gub_shards, member * part, axis=2
    )
    vectors = jnp.stack(
        [
            *[grt[e] for e in range(EXPERTS)],
            grad_qv[0],
            grad_qv[1],
            grad_gain_one,
            grad_bias_one,
            grad_gain_two,
            grad_bias_two,
            grad_out_bias,
            *[gdb[e] for e in range(EXPERTS)],
        ]
    )
    grad_small = jnp.concatenate(
        [
            vectors.T,
            gub_full.reshape(width, bias_columns),
            jnp.zeros((width, pad), F32),
        ],
        axis=1,
    )
    grad_packed = jnp.concatenate(
        [grad_qkv.astype(BF), grad_out.astype(BF), grad_small.astype(BF)], axis=1
    )
    total = reduce_dense(links, grad_packed)
    share = [total[:, offsets[i] : offsets[i + 1]] for i in range(len(sizes))]

    up_all = gather_quarters(links, part_up)
    down_all = gather_quarters(links, part_down)
    grad_up = jnp.transpose(up_all, (1, 3, 0, 2)).reshape(EXPERTS, width, ff_rows).astype(F32)
    grad_down = jnp.swapaxes(down_all, 0, 1).reshape(EXPERTS, ff_rows, width).astype(F32)
    return (
        mixed,
        grad_tokens,
        share[2][:, 0],
        share[3][:, 0],
        total[:, : 3 * width],
        share[1].T,
        total[:, 3 * width : 4 * width],
        share[6][:, 0],
        share[4][:, 0],
        share[5][:, 0],
        share[0],
        grad_up,
        share[8].reshape(EXPERTS, ff_rows),
        grad_down,
        share[7].T,
    )


def solution(mesh):
    links = Links(mesh.shape["shard"], mesh.shape["replica"])
    both = ("shard", "replica")
    return jax.shard_map(
        functools.partial(local, links),
        mesh=mesh,
        in_specs=(
            P(both, None, None),
            P(both, None, None),
            P(both),
            P(both, None, None),
            P("shard"),
            P("shard"),
            P("shard", None),
            P(None, "shard"),
            P("shard", None),
            P("shard"),
            P("shard"),
            P("shard"),
            P("shard", None),
            P(None, None, "shard"),
            P(None, "shard"),
            P(None, "shard", None),
            P(None, "shard"),
        ),
        out_specs=(
            P(both, None, None),
            P(both, None, None),
            P("shard"),
            P("shard"),
            P("shard", None),
            P(None, "shard"),
            P("shard", None),
            P("shard"),
            P("shard"),
            P("shard"),
            P("shard", None),
            P(None, None, "shard"),
            P(None, "shard"),
            P(None, "shard", None),
            P(None, "shard"),
        ),
        check_vma=False,
    )
```

```python
import functools
import math

import jax
import jax.numpy as jnp
from jax import lax
from jax.experimental import pallas as pl
from jax.experimental.pallas import tpu as pltpu
from jax.sharding import PartitionSpec as P

HEADS = 8
EXPERTS = 8
TOP = 2
NORM_EPS = 1e-06
TILE = 256
SEG = 16
PIECE = 64
CHUNK = 256
CAP = 376
GROUPS = 2
LANES = 128
BF = jnp.bfloat16
F32 = jnp.float32


SMALL_DOWN = 8
SMALL_QV = 16
SMALL_VEC = 18
SMALL_UP = 32


def cycle_order(count):
    if count % 2 or count < 4:
        return list(range(count))
    return list(range(0, count, 2)) + list(range(count - 1, 0, -2))


class Links:
    def __init__(self, shards, copies):
        self.shards, self.copies = shards, copies
        self.team = min(4, copies)
        self.halves = min(2, self.team)
        self.order = cycle_order(shards)
        self.place = [self.order.index(s) for s in range(shards)]
        ring = self.order + self.order[:1]
        self.ahead = [(ring[i], ring[i + 1]) for i in range(shards)]
        self.back = [(b, a) for a, b in self.ahead]
        self.team_bits = [1 << i for i in range(self.team.bit_length() - 1)]
        self.other_bits = []
        bit = self.team
        while bit < copies:
            self.other_bits.append(bit)
            bit *= 2

    def ring_ahead(self, value):
        return lax.ppermute(value, "shard", self.ahead)

    def ring_back(self, value):
        return lax.ppermute(value, "shard", self.back)

    def swap(self, value, bit):
        return lax.ppermute(value, "replica", [(i, i ^ bit) for i in range(self.copies)])

    def my_place(self):
        return jnp.asarray(self.place, jnp.int32)[lax.axis_index("shard")]

    def my_copy(self):
        return lax.axis_index("replica")

    def behind(self):
        step = jnp.mod(self.my_place() - jnp.arange(self.shards), self.shards)
        return jnp.asarray(self.order, jnp.int32)[step]

    def ahead_of(self):
        step = jnp.mod(self.my_place() + jnp.arange(self.shards), self.shards)
        return jnp.asarray(self.order, jnp.int32)[step]


def add_low(first, second):
    return (first.astype(F32) + second.astype(F32)).astype(BF)


def dot_nn(a, b):
    return lax.dot_general(a, b, (((1,), (0,)), ((), ())), preferred_element_type=F32)


def dot_nt(a, b):
    return lax.dot_general(a, b, (((1,), (1,)), ((), ())), preferred_element_type=F32)


def dot_tn(a, b):
    return lax.dot_general(a, b, (((0,), (0,)), ((), ())), preferred_element_type=F32)


def one_hot(rows, columns, offset):
    row = lax.broadcasted_iota(jnp.int32, (rows, columns), 0)
    column = lax.broadcasted_iota(jnp.int32, (rows, columns), 1)
    return jnp.where(column == row + offset, 1.0, 0.0).astype(BF)


def params(mib=None, steps=1):
    limit = None if mib is None else mib * 1024 * 1024
    return pltpu.CompilerParams(
        dimension_semantics=("arbitrary",) * steps, vmem_limit_bytes=limit
    )


def cost(flops, moved):
    return pl.CostEstimate(flops=int(flops), bytes_accessed=int(moved), transcendentals=0)


VMEM = pl.BlockSpec(memory_space=pltpu.VMEM)
ANY = pl.BlockSpec(memory_space=pl.ANY)
SMEM = pl.BlockSpec(memory_space=pltpu.SMEM)


def padded(tokens):
    return (tokens + 7) // 8 * 8


def keep_kernel(live, values, kept):
    for i in range(values.shape[0]):
        flag = jnp.where(live[0] > i, 1.0, 0.0).astype(BF)
        kept[i, 0 : values.shape[1], :] = values[i] * flag


def keep_live(live_images, values):
    width = values.shape[2]
    return pl.pallas_call(
        keep_kernel,
        in_specs=[SMEM, VMEM],
        out_specs=VMEM,
        out_shape=jax.ShapeDtypeStruct((values.shape[0], padded(values.shape[1]), width), BF),
        cost_estimate=cost(1e6, 4e6),
        name="keep_live",
    )(live_images, values)


def mixed_kernel(live, mid, own, other, far, mixed):
    total = own[...].astype(F32) + other[...].astype(F32) + far[...].astype(F32)
    tokens = mid.shape[1]
    flag = jnp.where(live[0] > pl.program_id(0), 1.0, 0.0)
    mixed[0] = ((mid[0] + total[0, 0:tokens, :]) * flag).astype(BF)


def finish_mixed(live_images, middle, parts):
    images, tokens, width = middle.shape
    row = pl.BlockSpec((1, tokens, width), lambda i: (i, 0, 0))
    part = pl.BlockSpec((1, padded(tokens), width), lambda i: (i, 0, 0))
    return pl.pallas_call(
        mixed_kernel,
        grid=(images,),
        in_specs=[SMEM, row, part, part, part],
        out_specs=row,
        out_shape=jax.ShapeDtypeStruct(middle.shape, BF),
        compiler_params=params(),
        cost_estimate=cost(4 * images * tokens * width, 12 * images * tokens * width),
        name="finish_mixed",
    )(live_images, middle, *parts)


def place_kernel(members, who, *refs):
    blocks, (up_out, down_out, both) = refs[:members], refs[-3:]
    part = blocks[0].shape[2]
    here = part * members
    for layer, target in ((0, up_out), (1, down_out)):
        for i in range(members):
            at = pl.ds(pl.multiple_of((who[0] ^ who[1 + i]) * part, part), part)
            both[at, :] = blocks[i][layer, 0].astype(F32)
        if layer:
            target[0] = both[...]
        else:
            target[0] = dot_tn(both[...].astype(BF), one_hot(here, here, 0))


def place_experts(links, blocks, start, before):
    _, experts, part, width = blocks[0].shape
    members = len(blocks)
    here = part * members
    flips = [0]
    for bit in reversed(links.team_bits):
        flips = flips + [f ^ bit for f in flips]
    member = (links.my_copy() % links.team).astype(jnp.int32).reshape(1)
    table = jnp.concatenate([member, jnp.asarray(flips, jnp.int32)])
    return pl.pallas_call(
        functools.partial(place_kernel, members),
        grid_spec=pltpu.PrefetchScalarGridSpec(
            num_scalar_prefetch=1,
            grid=(experts,),
            in_specs=[pl.BlockSpec((2, 1, part, width), lambda e, w: (0, e, 0, 0))] * members
            + [ANY] * len(before),
            out_specs=[
                pl.BlockSpec((1, width, here), lambda e, w: (start + e, 0, 0)),
                pl.BlockSpec((1, here, width), lambda e, w: (start + e, 0, 0)),
            ],
            scratch_shapes=[pltpu.VMEM((here, width), F32)],
        ),
        out_shape=[
            jax.ShapeDtypeStruct((EXPERTS, width, here), F32),
            jax.ShapeDtypeStruct((EXPERTS, here, width), F32),
        ],
        input_output_aliases={1 + members + i: i for i in range(len(before))},
        compiler_params=params(),
        cost_estimate=cost(2 * experts * here * here * width, 12 * experts * here * width),
        name="place_experts",
    )(table, *blocks, *before)


def pack_dense_kernel(
    who, qkv, out, router, qv_bias, g1, b1, g2, b2, ob, db, ub, mine, other, low, small
):
    columns = qkv.shape[1]
    half = mine.shape[0]
    halves = qkv.shape[0] // half
    for target, flip in ((mine, 0), (other, 1)):
        core = (who[0] ^ flip) if halves > 1 else 0
        at = pl.ds(pl.multiple_of(core * half, half), half)
        target[:, :columns] = qkv[at, :]
        target[:, columns:] = out[at, :]
    here = router.shape[0]
    rows = small.shape[0]
    eye = one_hot(here, here, 0)
    small[...] = jnp.zeros((rows, here), F32)
    small[0:EXPERTS, :] = dot_tn(router[...], eye)
    small[SMALL_DOWN : SMALL_DOWN + EXPERTS, :] = db[...].astype(F32)
    small[SMALL_QV : SMALL_QV + 2, :] = qv_bias[...].astype(F32)
    for i, v in enumerate((g1, b1, g2, b2, ob)):
        small[SMALL_VEC + i : SMALL_VEC + i + 1, :] = v[...].astype(F32)
    for c in range(ub.shape[1] // here):
        at = SMALL_UP + c * EXPERTS
        small[at : at + EXPERTS, :] = ub[:, c * here : (c + 1) * here].astype(F32)
    low[...] = small[...].astype(BF)


def pack_dense(links, weights):
    qkv, out, router, qv, g1, b1, g2, b2, ob, db, ub = weights
    here, columns = qkv.shape
    rows = SMALL_UP + ub.shape[1] // here * EXPERTS
    vectors = [v.reshape(1, here) for v in (g1, b1, g2, b2, ob)]
    rest = [router, qv, *vectors, db, ub]
    width = columns + out.shape[1]
    half = here // links.halves
    who = (links.my_copy() % links.halves).astype(jnp.int32).reshape(1)
    return pl.pallas_call(
        pack_dense_kernel,
        in_specs=[SMEM] + [VMEM] * (2 + len(rest)),
        out_specs=[VMEM] * 3,
        out_shape=[
            jax.ShapeDtypeStruct((half, width), BF),
            jax.ShapeDtypeStruct((half, width), BF),
            jax.ShapeDtypeStruct((rows, here), BF),
        ],
        scratch_shapes=[pltpu.VMEM((rows, here), F32)],
        cost_estimate=cost(1e6, 1e6),
        name="pack_dense",
    )(who, qkv, out, *rest)


def pack_experts_kernel(who, up, down, packed):
    part = packed.shape[2]
    offset = who[0] * part % up.shape[2]
    packed[0, 0] = dot_nt(one_hot(part, up.shape[2], offset), up[0]).astype(BF)
    packed[1, 0] = down[0]


def pack_experts(links, up, down, start, count):
    width, here = up.shape[1:]
    part = here // links.team
    lanes = min(LANES, here)
    who = (links.my_copy() % links.team).astype(jnp.int32).reshape(1)
    return pl.pallas_call(
        pack_experts_kernel,
        grid_spec=pltpu.PrefetchScalarGridSpec(
            num_scalar_prefetch=1,
            grid=(count,),
            in_specs=[
                pl.BlockSpec((1, width, lanes), lambda g, w: (start + g, 0, w[0] * part // lanes)),
                pl.BlockSpec((1, part, width), lambda g, w: (start + g, w[0], 0)),
            ],
            out_specs=pl.BlockSpec((2, 1, part, width), lambda g, w: (0, g, 0, 0)),
        ),
        out_shape=jax.ShapeDtypeStruct((2, count, part, width), BF),
        compiler_params=params(),
        cost_estimate=cost(2 * count * part * width * lanes, 6 * count * part * width),
        name="pack_experts",
    )(who, up, down)


def unpack_kernel(shards, table, *refs):
    smalls = refs[:shards]
    vec, router, down_bias, up_ring, ring = refs[shards:]
    rows, here = smalls[0].shape
    width = shards * here
    total = jnp.zeros((rows, width), F32)
    behind = jnp.zeros((rows, width), F32)
    for j in range(shards):
        piece = smalls[j][...]
        total = total + dot_nn(piece, one_hot(here, width, table[j] * here))
        behind = behind + dot_nn(piece, one_hot(here, width, j * here))
    ring[...] = behind
    router[...] = jnp.zeros(router.shape, BF)
    row = lax.broadcasted_iota(jnp.int32, (16, width), 0)
    router[0:16, :] = jnp.where(row < EXPERTS, total[0:16, :], 0.0).astype(BF)
    down_bias[...] = total[SMALL_DOWN : SMALL_DOWN + EXPERTS, :]
    vec[0:2, :] = total[SMALL_VEC : SMALL_VEC + 2, :]
    vec[2:4, :] = total[SMALL_QV : SMALL_QV + 2, :]
    vec[4:5, :] = total[SMALL_VEC + 4 : SMALL_VEC + 5, :]
    vec[5:7, :] = total[SMALL_VEC + 2 : SMALL_VEC + 4, :]
    vec[7:8, :] = jnp.zeros((1, width), F32)
    at = pl.multiple_of(SMALL_UP + table[shards] * EXPERTS, 8)
    up_ring[...] = ring[pl.ds(at, EXPERTS), :]


def unpack_small(links, smalls):
    rows, here = smalls[0].shape
    width = here * links.shards
    member = (links.my_copy() % links.team).astype(jnp.int32).reshape(1)
    table = jnp.concatenate([links.behind(), member])
    return pl.pallas_call(
        functools.partial(unpack_kernel, links.shards),
        in_specs=[pl.BlockSpec(memory_space=pltpu.SMEM), *[VMEM] * links.shards],
        out_specs=[VMEM] * 4,
        out_shape=[
            jax.ShapeDtypeStruct((8, width), F32),
            jax.ShapeDtypeStruct((LANES, width), BF),
            jax.ShapeDtypeStruct((EXPERTS, width), F32),
            jax.ShapeDtypeStruct((EXPERTS, width), F32),
        ],
        scratch_shapes=[pltpu.VMEM((rows, width), F32)],
        cost_estimate=cost(4 * rows * width * width, 4 * rows * width),
        name="unpack_small",
    )(table, *smalls)


def route_kernel(experts_held, *refs):
    blocks, (positions, tables, ranks) = refs[:-3], refs[-3:]
    held, _, tokens = blocks[0].shape
    images = held * len(blocks)
    groups = EXPERTS // experts_held
    none = 1023.0
    routes = [
        jnp.concatenate([b[:, k, :] for b in blocks], axis=0).astype(F32) for k in range(TOP)
    ]
    lane = lax.broadcasted_iota(jnp.int32, (images, LANES), 1)
    row = lax.broadcasted_iota(jnp.int32, (tokens, tokens), 0)
    column = lax.broadcasted_iota(jnp.int32, (tokens, tokens), 1)
    earlier = jnp.where(row < column, 1.0, 0.0).astype(BF)
    count = jnp.zeros((images, LANES), F32)
    for e in range(EXPERTS):
        hot = jnp.where((routes[0] == e) | (routes[1] == e), 1.0, 0.0)
        ranks[e] = dot_nn(hot.astype(BF), earlier)
        count = jnp.where(lane == e, jnp.sum(hot, axis=1, keepdims=True), count)
    padded = ((count.astype(jnp.int32) + (SEG - 1)) // SEG) * SEG
    pieces = (padded + (PIECE - 1)) // PIECE
    padded_low = padded.astype(F32).astype(BF)
    a = lax.broadcasted_iota(jnp.int32, (LANES, LANES), 0)
    b = lax.broadcasted_iota(jnp.int32, (LANES, LANES), 1)
    same = (a // experts_held == b // experts_held) & (a < b) & (b < EXPERTS)
    same = jnp.where(same, 1.0, 0.0).astype(BF)
    local_start = dot_nn(padded_low, same)
    a = lax.broadcasted_iota(jnp.int32, (images, images), 0)
    b = lax.broadcasted_iota(jnp.int32, (images, images), 1)
    above = dot_nn(jnp.where(b < a, 1.0, 0.0).astype(BF), padded_low)
    used = jnp.sum(padded.astype(F32), axis=0, keepdims=True)
    tiles = (used.astype(jnp.int32) + (PIECE - SEG + TILE - 1)) // TILE
    tiles_low = jnp.broadcast_to(tiles, (8, LANES)).astype(F32).astype(BF)
    start = dot_nn(tiles_low, same)[0:1] * TILE
    tables[...] = jnp.zeros_like(tables)
    tables[0:images] = local_start.astype(jnp.int32)
    tables[images : 2 * images] = (above + start).astype(jnp.int32)
    tables[2 * images : 3 * images] = pieces
    tables[3 * images : 3 * images + 1] = start.astype(jnp.int32)
    tables[3 * images + 1 : 3 * images + 2] = tiles
    tables[3 * images + 2 : 3 * images + 3] = used.astype(jnp.int32)
    for g in range(groups):
        for k in range(TOP):
            pos = jnp.full((images, tokens), none, F32)
            for e in range(g * experts_held, (g + 1) * experts_held):
                first = jnp.sum(jnp.where(lane == e, local_start, 0.0), axis=1, keepdims=True)
                pos = jnp.where(routes[k] == e, ranks[e] + first, pos)
            positions[g, k] = pos.astype(jnp.int32)


def route_tables(blocks, experts_held):
    held, _, tokens = blocks[0].shape
    images = held * len(blocks)
    groups = EXPERTS // experts_held
    return pl.pallas_call(
        functools.partial(route_kernel, experts_held),
        in_specs=[VMEM] * len(blocks),
        out_specs=[VMEM] * 2,
        out_shape=[
            jax.ShapeDtypeStruct((groups, TOP, images, tokens), jnp.int32),
            jax.ShapeDtypeStruct((3 * images + 8, LANES), jnp.int32),
        ],
        scratch_shapes=[pltpu.VMEM((EXPERTS, images, tokens), F32)],
        cost_estimate=cost(2e7, 1e6),
        name="route_tables",
    )(*blocks)


def begin(copies):
    for c in copies:
        c.start()


def finish(copies):
    for c in copies:
        c.wait()


def token_copies(sources, buffer, sems, slot, first_sem):
    copies, at = [], 0
    for p, source in enumerate(sources):
        size = source.shape[0]
        copies.append(
            pltpu.make_async_copy(
                source, buffer.at[slot, pl.ds(at, size)], sems.at[slot, first_sem + p]
            )
        )
        at += size
    return copies


def row_copies(count, first_row, sources, targets, sems, act):
    def one(k, carry):
        rows = pl.ds(pl.multiple_of(first_row + k * TILE, TILE), TILE)
        for i, (source, target) in enumerate(zip(sources, targets)):
            copy = pltpu.make_async_copy(source.at[rows], target.at[rows], sems[i])
            if act == "start":
                copy.start()
            else:
                copy.wait()
        return carry

    lax.fori_loop(0, count, one, 0)


def dispatch_kernel(dims, meta, *refs):
    members, held, pieces, tokens = dims
    hids = [refs[p * members : (p + 1) * members] for p in range(pieces)]
    refs = refs[pieces * members :]
    cots, refs = refs[:members], refs[members:]
    posr, router, x_out, t_out, a_out, probs_out = refs[:6]
    xb, tb, ax, xt, tt, at, hbuf, cbuf, token_sems, out_sems = refs[6:]
    step = pl.program_id(0)
    slots = xt.shape[1] - PIECE
    width = cbuf.shape[3]
    images = members * held
    lane = lax.broadcasted_iota(jnp.int32, (1, LANES), 1)

    def fetch(m):
        slot = m % 2
        return token_copies([h[m] for h in hids], hbuf, token_sems, slot, 0) + token_copies(
            [cots[m]], cbuf, token_sems, slot, pieces
        )

    @pl.when(step == 0)
    def _():
        begin(fetch(0))
        xt[...] = jnp.zeros_like(xt)
        tt[...] = jnp.zeros_like(tt)
        at[...] = jnp.zeros_like(at)

    for m in range(members):

        @pl.when(step == m)
        def _(m=m):
            finish(fetch(m))
            if m + 1 < members:
                begin(fetch(m + 1))

    slot = step % 2
    row = lax.broadcasted_iota(jnp.int32, (slots, tokens), 0)
    for i in range(held):
        image = step * held + i
        h = hbuf[slot, i, 0:tokens, :]
        c = cbuf[slot, i, 0:tokens, :]
        logits = dot_nt(h, router[...])
        logits = jnp.where(lane < EXPERTS, logits, -1e30)
        e = jnp.exp(logits - jnp.max(logits, axis=1, keepdims=True))
        probs = e / jnp.sum(e, axis=1, keepdims=True)
        probs_out[i] = probs
        high = probs.astype(BF)
        low = (probs - high.astype(F32)).astype(BF)
        first = posr[0, 0, pl.ds(image, 1), :]
        second = posr[0, 1, pl.ds(image, 1), :]
        pick = jnp.where((row == first) | (row == second), 1.0, 0.0).astype(BF)
        xt[i, 0:slots, :] = dot_nn(pick, h).astype(BF)
        tt[i, 0:slots, :] = dot_nn(pick, c).astype(BF)
        at[i, 0:slots, :] = dot_nn(pick, high) + dot_nn(pick, low)
    for i in range(held):
        image = step * held + i
        for e in range(EXPERTS):
            src = meta[image, e]
            dst = meta[images + image, e]

            def copy(k, carry, src=src, dst=dst, i=i):
                s = pl.ds(pl.multiple_of(src + k * PIECE, SEG), PIECE)
                d = pl.ds(pl.multiple_of(dst + k * PIECE, SEG), PIECE)
                xb[d, :] = xt[i, s, :]
                tb[d, :] = tt[i, s, :]
                ax[d, :] = at[i, s, :]
                return carry

            lax.fori_loop(0, meta[2 * images + image, e], copy, 0)

    @pl.when(step == members - 1)
    def _():
        sems = [out_sems.at[i] for i in range(3)]
        held_rows, sent_rows = (xb, tb, ax), (x_out, t_out, a_out)
        total = jnp.int32(0)
        for e in range(EXPERTS):
            start = meta[3 * images, e]
            tiles = meta[3 * images + 1, e]
            used = meta[3 * images + 2, e]

            def clear(k, carry, start=start, used=used):
                d = pl.ds(pl.multiple_of(start + used + k * SEG, SEG), SEG)
                xb[d, :] = jnp.zeros((SEG, width), BF)
                tb[d, :] = jnp.zeros((SEG, width), BF)
                ax[d, :] = jnp.zeros((SEG, LANES), F32)
                return carry

            lax.fori_loop(0, (tiles * TILE - used) // SEG, clear, 0)
            row_copies(tiles, start, held_rows, sent_rows, sems, "start")
            total = total + tiles
        row_copies(total, 0, held_rows, sent_rows, sems, "wait")


def row_bound(tokens, images, members):
    most = min(EXPERTS * CAP * members, TOP * tokens * images) + images * EXPERTS * (SEG - 1)
    rows = most + EXPERTS * (PIECE + TILE)
    return (rows + TILE - 1) // TILE * TILE


def slot_bound(tokens):
    return (TOP * tokens + (SEG - 1) * EXPERTS + PIECE - 1) // PIECE * PIECE


def whole_spec(shape):
    return pl.BlockSpec(tuple(shape), lambda s, *_: (0,) * len(shape))


def dispatch(hids, cots, positions, meta, router):
    members = len(cots)
    held, token_rows, width = cots[0].shape
    tokens = positions.shape[3]
    pieces = len(hids)
    images = members * held
    rows, slots = row_bound(tokens, images, members), slot_bound(tokens)
    shapes = [
        jax.ShapeDtypeStruct((rows, width), BF),
        jax.ShapeDtypeStruct((rows, width), BF),
        jax.ShapeDtypeStruct((rows, LANES), F32),
    ]
    return pl.pallas_call(
        functools.partial(dispatch_kernel, (members, held, pieces, tokens)),
        grid_spec=pltpu.PrefetchScalarGridSpec(
            num_scalar_prefetch=1,
            grid=(members,),
            in_specs=[
                *[ANY] * (members * (pieces + 1)),
                whole_spec(positions.shape),
                whole_spec(router.shape),
            ],
            out_specs=[
                ANY,
                ANY,
                ANY,
                pl.BlockSpec((held, tokens, LANES), lambda s, m: (s, 0, 0)),
            ],
            scratch_shapes=[
                *[pltpu.VMEM(a.shape, a.dtype) for a in shapes],
                pltpu.VMEM((held, slots + PIECE, width), BF),
                pltpu.VMEM((held, slots + PIECE, width), BF),
                pltpu.VMEM((held, slots + PIECE, LANES), F32),
                pltpu.VMEM((2, held, token_rows, width), BF),
                pltpu.VMEM((2, held, token_rows, width), BF),
                pltpu.SemaphoreType.DMA((2, pieces + 1)),
                pltpu.SemaphoreType.DMA((3,)),
            ],
        ),
        out_shape=[*shapes, jax.ShapeDtypeStruct((images, tokens, LANES), F32)],
        compiler_params=params(60),
        cost_estimate=cost(6 * images * slots * tokens * width, 5 * rows * width),
        name="dispatch",
    )(meta, *[b for piece in hids for b in piece], *cots, positions, router)


def expert_kernel(dims, meta, *refs):
    images, experts, chunks, team, first_expert, offset = dims
    x_in, t_in, a_in, up_bias, down_bias = refs[:5]
    weights, refs = refs[5 : 6 + chunks], refs[6 + chunks :]
    x_out, t_out, a_out, grads, gub, gdb = refs[:6]
    xb, tb, ax, wbuf, gu_acc, gd_acc, gb_acc, db_acc, sems, row_sems = refs[6:]
    step = pl.program_id(0)
    part = wbuf.shape[2] // chunks
    lane = lax.broadcasted_iota(jnp.int32, (1, LANES), 1)

    def weight_copies(e, slot):
        copies = []
        for j in range(chunks):
            for layer in range(2):
                if j < chunks // 2:
                    source = weights[j].at[layer, offset + e]
                elif j == chunks // 2:
                    source = weights[j + layer].at[offset + e]
                else:
                    source = weights[j + 1].at[layer, offset + e]
                copies.append(
                    pltpu.make_async_copy(
                        source,
                        wbuf.at[slot, layer, pl.ds(j * part, part)],
                        sems.at[slot, 2 * j + layer],
                    )
                )
        return copies

    def fetched(e, act):
        start = meta[3 * images, first_expert + e]
        tiles = meta[3 * images + 1, first_expert + e]
        own = [row_sems.at[e % 2, i] for i in range(3)]
        row_copies(tiles, start, (x_in, t_in, a_in), (xb, tb, ax), own, act)

    @pl.when(step == 0)
    def _():
        begin(weight_copies(0, 0))
        fetched(0, "start")

    e = step
    slot = e % 2
    name = first_expert + e
    start = meta[3 * images, name]
    tiles = meta[3 * images + 1, name]
    fetched(e, "wait")
    finish(weight_copies(e, slot))

    @pl.when(e + 1 < experts)
    def _():
        begin(weight_copies(e + 1, 1 - slot))
        fetched(e + 1, "start")

    gu_acc[...] = jnp.zeros_like(gu_acc)
    gd_acc[...] = jnp.zeros_like(gd_acc)
    gb_acc[...] = jnp.zeros_like(gb_acc)
    db_acc[...] = jnp.zeros_like(db_acc)
    wu = wbuf.at[slot, 0]
    wd = wbuf.at[slot, 1]
    bias = up_bias[pl.ds(name, 1), :]
    second_bias = down_bias[pl.ds(name, 1), :] * (1.0 / team)
    mine = lane == name

    def tile(at_row, size):
        here = pl.ds(pl.multiple_of(at_row, SEG), size)
        x = xb[here, :]
        t = tb[here, :]
        gate = jnp.sum(jnp.where(mine, ax[here, :], 0.0), axis=1, keepdims=True)
        pre = dot_nt(x, wu[...]) + bias
        u = 1.0 / (1.0 + (0.3275911 * math.sqrt(0.5)) * jnp.abs(pre))
        bell = jnp.exp(-0.5 * pre * pre)
        poly = 0.5 * 1.421413741 + u * (-0.5 * 1.453152027 + u * (0.5 * 1.061405429))
        poly = u * (0.5 * 0.254829592 + u * (-0.5 * 0.284496736 + u * poly))
        half = poly * bell
        phi = jnp.where(pre >= 0, 1.0 - half, half)
        active = (pre * phi).astype(BF)
        active_float = active.astype(F32)
        slope = phi + pre * bell * (1.0 / math.sqrt(2.0 * math.pi))
        raw = dot_nt(t, wd[...])
        t_float = t.astype(F32)
        score = jnp.sum(active_float * raw, axis=1, keepdims=True) + jnp.sum(
            t_float * second_bias, axis=1, keepdims=True
        )
        gated = (gate * active_float).astype(BF)
        dpre = (gate * raw) * slope
        gb_acc[...] += jnp.sum(dpre, axis=0, keepdims=True)
        db_acc[...] += jnp.sum(gate * t_float, axis=0, keepdims=True)
        dpre = dpre.astype(BF)
        gd_acc[...] += dot_tn(gated, t)
        gu_acc[...] += dot_tn(dpre, x)
        xb[here, :] = (dot_nn(gated, wd[...]) + gate * second_bias).astype(BF)
        tb[here, :] = dot_nn(dpre, wu[...]).astype(BF)
        ax[here, :] = jnp.where(mine, score, 0.0)

    def pair(k, carry):
        tile(start + k * (2 * TILE), 2 * TILE)
        return carry

    lax.fori_loop(0, tiles // 2, pair, 0)

    @pl.when(tiles % 2 == 1)
    def _():
        tile(start + (tiles - 1) * TILE, TILE)

    for j in range(chunks):
        rows = slice(j * part, (j + 1) * part)
        grads[j, 0, 0] = gu_acc[rows, :].astype(BF)
        grads[j, 1, 0] = gd_acc[rows, :].astype(BF)
    gub[pl.ds(e, 1), :] = gb_acc[...]
    gdb[pl.ds(e, 1), :] = db_acc[...] * (1.0 / team)
    out = ((xb, tb, ax), (x_out, t_out, a_out), [row_sems.at[2, i] for i in range(3)])
    row_copies(tiles, start, *out, "start")

    @pl.when(e + 1 == experts)
    def _():
        first = meta[3 * images, first_expert]
        row_copies((start - first) // TILE + tiles, first, *out, "wait")


def expert_call(links, rows, weights, up_bias, down_bias, meta, group, experts):
    team, shards = links.team, links.shards
    part, width = weights[0].shape[-2:]
    hidden = part * shards
    images = (meta.shape[0] - 8) // 3
    dims = (images, experts, shards, team, group * experts, group * experts)
    return pl.pallas_call(
        functools.partial(expert_kernel, dims),
        grid_spec=pltpu.PrefetchScalarGridSpec(
            num_scalar_prefetch=1,
            grid=(experts,),
            in_specs=[ANY, ANY, ANY, whole_spec(up_bias.shape), whole_spec(down_bias.shape)]
            + [ANY] * len(weights),
            out_specs=[
                ANY,
                ANY,
                ANY,
                pl.BlockSpec((shards, 2, 1, part, width), lambda s, m: (0, 0, s, 0, 0)),
                whole_spec((experts, hidden)),
                whole_spec((experts, width)),
            ],
            scratch_shapes=[
                *[pltpu.VMEM(a.shape, a.dtype) for a in rows],
                pltpu.VMEM((2, 2, hidden, width), BF),
                pltpu.VMEM((hidden, width), F32),
                pltpu.VMEM((hidden, width), F32),
                pltpu.VMEM((1, hidden), F32),
                pltpu.VMEM((1, width), F32),
                pltpu.SemaphoreType.DMA((2, 2 * shards)),
                pltpu.SemaphoreType.DMA((3, 3)),
            ],
        ),
        out_shape=[
            *[jax.ShapeDtypeStruct(a.shape, a.dtype) for a in rows],
            jax.ShapeDtypeStruct((shards, 2, experts, part, width), BF),
            jax.ShapeDtypeStruct((experts, hidden), F32),
            jax.ShapeDtypeStruct((experts, width), F32),
        ],
        compiler_params=params(60),
        cost_estimate=cost(
            12 * rows[0].shape[0] // GROUPS * hidden * width, 8 * experts * hidden * width
        ),
        name="experts",
    )(meta, *rows, up_bias, down_bias, *weights)


def combine_kernel(dims, meta, *refs):
    members, held, pieces, size = dims
    done, refs = refs[: 3 * GROUPS], refs[3 * GROUPS :]
    hids = [refs[p * members : (p + 1) * members] for p in range(pieces)]
    refs = refs[pieces * members :]
    posr, probs_in, router = refs[:3]
    mix_keep, mix_give, dhid_keep, dhid_give, grt = refs[3:8]
    xb, tb, ax, xt, tt, at, hbuf, posc, token_sems, done_sems = refs[8:]
    step = pl.program_id(0)
    images = members * held
    tokens = posr.shape[3]
    slots = xt.shape[1] - PIECE

    def fetch_tokens(m):
        return token_copies([h[m] for h in hids], hbuf, token_sems, m % 2, 0)

    def fetch_rows(act):
        for g in range(GROUPS):
            start = meta[3 * images, g * size]
            last = g * size + size - 1
            end = meta[3 * images, last] // TILE + meta[3 * images + 1, last]
            sems = [done_sems.at[g, i] for i in range(3)]
            row_copies(end - start // TILE, start, done[3 * g : 3 * g + 3], (xb, tb, ax), sems, act)

    @pl.when(step == 0)
    def _():
        fetch_rows("start")
        begin(fetch_tokens(0))
        grt[...] = jnp.zeros_like(grt)
        xt[...] = jnp.zeros_like(xt)
        tt[...] = jnp.zeros_like(tt)
        at[...] = jnp.zeros_like(at)
        eye = one_hot(images, images, 0)
        for k in range(TOP):
            pos = posr[0, k]
            high = (pos // 16).astype(F32).astype(BF)
            low = (pos % 16).astype(F32).astype(BF)
            posc[k] = (dot_tn(high, eye) * 16.0 + dot_tn(low, eye)).astype(jnp.int32)
        fetch_rows("wait")

    for m in range(members):

        @pl.when(step == m)
        def _(m=m):
            finish(fetch_tokens(m))
            if m + 1 < members:
                begin(fetch_tokens(m + 1))

    m = step
    slot = m % 2
    for i in range(held):
        image = m * held + i
        for e in range(EXPERTS):
            dst = meta[image, e]
            src = meta[images + image, e]

            def copy(k, carry, src=src, dst=dst, i=i):
                s = pl.ds(pl.multiple_of(src + k * PIECE, SEG), PIECE)
                d = pl.ds(pl.multiple_of(dst + k * PIECE, SEG), PIECE)
                xt[i, d, :] = xb[s, :]
                tt[i, d, :] = tb[s, :]
                at[i, d, :] = ax[s, :]
                return carry

            lax.fori_loop(0, meta[2 * images + image, e], copy, 0)
    total = jnp.zeros(grt.shape, F32)
    keeps = m < members // 2
    column = lax.broadcasted_iota(jnp.int32, (1, images), 1)
    slot_of = lax.broadcasted_iota(jnp.int32, (tokens, slots), 1)
    for i in range(held):
        image = m * held + i
        h = hbuf[slot, i, 0:tokens, :]
        probs = probs_in[i]
        here = column == image
        back = None
        for k in range(TOP):
            pos = jnp.sum(jnp.where(here, posc[k], 0), axis=1, keepdims=True)
            back = (slot_of == pos) if back is None else back | (slot_of == pos)
        back = jnp.where(back, 1.0, 0.0).astype(BF)
        scores = at[i, 0:slots, :]
        high = scores.astype(BF)
        low = (scores - high.astype(F32)).astype(BF)
        mixture = dot_nn(back, xt[i, 0:slots, :])
        dprobs = dot_nn(back, high) + dot_nn(back, low)
        dlogits = probs * (dprobs - jnp.sum(dprobs * probs, axis=1, keepdims=True))
        dlogits = dlogits.astype(BF)
        dh = dot_nn(back, tt[i, 0:slots, :]) + dot_nn(dlogits, router[...])
        total = total + dot_tn(dlogits, h)
        xt[i, 0:tokens, :] = mixture.astype(BF)
        tt[i, 0:tokens, :] = dh.astype(BF)
    grt[...] += total

    @pl.when(keeps)
    def _():
        mix_keep[:, 0:tokens, :] = xt[:, 0:tokens, :]
        dhid_keep[:, 0:tokens, :] = tt[:, 0:tokens, :]

    @pl.when(jnp.logical_not(keeps))
    def _():
        mix_give[:, 0:tokens, :] = xt[:, 0:tokens, :]
        dhid_give[:, 0:tokens, :] = tt[:, 0:tokens, :]


def combine(done, hids, positions, probs, router, meta, size):
    pieces, members = len(hids), len(hids[0])
    images, tokens, _ = probs.shape
    width = router.shape[1]
    held = images // members
    slots = slot_bound(tokens)
    half = max(1, members // 2)
    token_rows = padded(tokens)
    token_block = (held, token_rows, width)
    keep = pl.BlockSpec(token_block, lambda s, m: (jnp.clip(s, 0, half - 1), 0, 0))
    give = pl.BlockSpec(token_block, lambda s, m: (jnp.clip(s - half, 0, half - 1), 0, 0))
    out_token = jax.ShapeDtypeStruct((half * held, token_rows, width), BF)
    return pl.pallas_call(
        functools.partial(combine_kernel, (members, held, pieces, size)),
        grid_spec=pltpu.PrefetchScalarGridSpec(
            num_scalar_prefetch=1,
            grid=(members,),
            in_specs=[ANY] * (3 * GROUPS + pieces * members)
            + [
                whole_spec(positions.shape),
                pl.BlockSpec((held, tokens, LANES), lambda s, m: (s, 0, 0)),
                whole_spec(router.shape),
            ],
            out_specs=[keep, give, keep, give, whole_spec((LANES, width))],
            scratch_shapes=[
                *[pltpu.VMEM(a.shape, a.dtype) for a in done[0]],
                pltpu.VMEM((held, slots + PIECE, width), BF),
                pltpu.VMEM((held, slots + PIECE, width), BF),
                pltpu.VMEM((held, slots + PIECE, LANES), F32),
                pltpu.VMEM((2, held, token_rows, width), BF),
                pltpu.VMEM((TOP, tokens, images), jnp.int32),
                pltpu.SemaphoreType.DMA((2, pieces)),
                pltpu.SemaphoreType.DMA((GROUPS, 3)),
            ],
        ),
        out_shape=[out_token] * 4 + [jax.ShapeDtypeStruct((LANES, width), F32)],
        compiler_params=params(60),
        cost_estimate=cost(6 * images * slots * tokens * width, 10 * images * slots * width),
        name="combine",
    )(
        meta,
        *[a for d in done for a in d],
        *[b for piece in hids for b in piece],
        positions,
        probs,
        router,
    )


def normalize(values):
    centered = values - jnp.mean(values, axis=-1, keepdims=True)
    scale = lax.rsqrt(jnp.mean(centered * centered, axis=-1, keepdims=True) + NORM_EPS)
    return centered * scale, scale


def normalize_back(incoming, gain, xhat, scale):
    g = incoming * gain
    first = jnp.mean(g, axis=-1, keepdims=True)
    second = jnp.mean(g * xhat, axis=-1, keepdims=True)
    return scale * (g - first - xhat * second)


def head_masks(head_size):
    lane = lax.broadcasted_iota(jnp.int32, (1, LANES), 1)
    return [lane // head_size == i for i in range(LANES // head_size)]


def fetch_weights(table, sources, weights, sems):
    copies = []
    for j, source in enumerate(sources):
        rows = source.shape[0]
        at = pl.multiple_of(table[j], rows)
        copies.append(pltpu.make_async_copy(source, weights.at[pl.ds(at, rows)], sems.at[j]))
    return copies


def forward_kernel(
    head_size, blocks, table, tokens, vec, *refs
):
    sources = refs[:blocks]
    first, qkv, att, mid, lse, hid, weights, sems = refs[blocks:]
    width = tokens.shape[2]
    qkv_w = weights.at[:, : 3 * width]
    out_w = weights.at[:, 3 * width :]

    @pl.when(pl.program_id(0) == 0)
    def _():
        copies = fetch_weights(table, sources, weights, sems)
        for c in copies:
            c.start()
        for c in copies:
            c.wait()

    x = tokens[0].astype(F32)
    xhat, _ = normalize(x)
    first_in = (xhat * vec[0:1, :] + vec[1:2, :]).astype(BF)
    first[0] = first_in
    projected = dot_nn(first_in, qkv_w[...])
    qkv[0, :, :width] = (projected[:, :width] + vec[2:3, :]).astype(BF)
    qkv[0, :, width : 2 * width] = projected[:, width : 2 * width].astype(BF)
    qkv[0, :, 2 * width :] = (projected[:, 2 * width :] + vec[3:4, :]).astype(BF)
    masks = head_masks(head_size)
    totals = jnp.zeros((x.shape[0], LANES), F32)
    lane = lax.broadcasted_iota(jnp.int32, (1, LANES), 1)
    for p in range(width // LANES):
        at = p * LANES
        q = qkv[0, :, at : at + LANES]
        k = qkv[0, :, width + at : width + at + LANES]
        v = qkv[0, :, 2 * width + at : 2 * width + at + LANES]
        out = None
        for i, mask in enumerate(masks):
            scores = dot_nt(jnp.where(mask, q, jnp.zeros_like(q)), k) * head_size ** (-0.5)
            top = jnp.max(scores, axis=-1, keepdims=True)
            e = jnp.exp(scores - top)
            total = jnp.sum(e, axis=-1, keepdims=True)
            soft = (e * (1.0 / total)).astype(BF)
            part = dot_nn(soft, v)
            out = part if out is None else jnp.where(mask, part, out)
            totals = jnp.where(lane == p * len(masks) + i, top + jnp.log(total), totals)
        att[0, :, at : at + LANES] = out.astype(BF)
    lse[0] = totals
    middle = x + (dot_nn(att[0], out_w[...]) + vec[4:5, :])
    mid[0] = middle
    xhat, _ = normalize(middle)
    hid[0, 0 : x.shape[0], :] = (xhat * vec[5:6, :] + vec[6:7, :]).astype(BF)


def backward_kernel(head_size, blocks, table, tokens, qkv, mid, lse, own, other, far, cot, vec, *refs):
    sources = refs[:blocks]
    dproj, dbranch, dtok, sums, datt, weights, sems = refs[blocks:]
    width = tokens.shape[2]
    qkv_w = weights.at[:, : 3 * width]
    out_w = weights.at[:, 3 * width :]
    scale_factor = head_size ** (-0.5)

    @pl.when(pl.program_id(0) == 0)
    def _():
        copies = fetch_weights(table, sources, weights, sems)
        for c in copies:
            c.start()
        for c in copies:
            c.wait()

    xhat, scale = normalize(mid[0])
    here = slice(0, tokens.shape[1])
    dhidden = own[0, here, :].astype(F32) + other[0, here, :].astype(F32)
    dhidden = dhidden + far[0, here, :].astype(F32)
    dmiddle = cot[0, here, :].astype(F32) + normalize_back(dhidden, vec[5:6, :], xhat, scale)
    branch = dmiddle.astype(BF)
    dbranch[0] = branch

    def column_sum(v):
        return jnp.sum(v, axis=0, keepdims=True)

    sums[0, 0:1, :] = column_sum(dhidden * xhat)
    sums[0, 1:2, :] = column_sum(dhidden)
    sums[0, 2:3, :] = column_sum(branch.astype(F32))
    datt[...] = dot_nt(branch, out_w[...]).astype(BF)
    masks = head_masks(head_size)
    lane = lax.broadcasted_iota(jnp.int32, (1, LANES), 1)
    for p in range(width // LANES):
        at = p * LANES
        q = qkv[0, :, at : at + LANES]
        k = qkv[0, :, width + at : width + at + LANES]
        v = qkv[0, :, 2 * width + at : 2 * width + at + LANES]
        do = datt[:, at : at + LANES]
        dq = dk = dv = None
        for i, mask in enumerate(masks):
            zero = jnp.zeros_like(q)
            here = lane == p * len(masks) + i
            total = jnp.sum(jnp.where(here, lse[0], 0.0), axis=-1, keepdims=True)
            soft = jnp.exp(dot_nt(jnp.where(mask, q, zero), k) * scale_factor - total)
            soft_low = soft.astype(BF)
            dsoft = dot_nt(jnp.where(mask, do, zero), v)
            ds = soft * (dsoft - jnp.sum(dsoft * soft, axis=-1, keepdims=True))
            ds = ds.astype(BF)
            dv_part = dot_tn(soft_low, do)
            dq_part = dot_nn(ds, k)
            dk_part = dot_tn(ds, q)
            dv = dv_part if dv is None else jnp.where(mask, dv_part, dv)
            dq = dq_part if dq is None else jnp.where(mask, dq_part, dq)
            dk = dk_part if dk is None else jnp.where(mask, dk_part, dk)
        dproj[0, :, at : at + LANES] = (dq * scale_factor).astype(BF)
        dproj[0, :, width + at : width + at + LANES] = (dk * scale_factor).astype(BF)
        dproj[0, :, 2 * width + at : 2 * width + at + LANES] = dv.astype(BF)
    sums[0, 3:4, :] = column_sum(dproj[0, :, :width].astype(F32))
    sums[0, 4:5, :] = column_sum(dproj[0, :, 2 * width :].astype(F32))
    dfirst = dot_nt(dproj[0], qkv_w[...])
    xhat, scale = normalize(tokens[0].astype(F32))
    sums[0, 5:6, :] = column_sum(dfirst * xhat)
    sums[0, 6:7, :] = column_sum(dfirst)
    sums[0, 7:8, :] = jnp.zeros((1, width), F32)
    dtok[0] = (dmiddle + normalize_back(dfirst, vec[0:1, :], xhat, scale)).astype(BF)


def attention_specs(seq_len, width, start, kinds):
    def row(columns):
        return pl.BlockSpec((1, seq_len, columns), lambda g, t: (g + start, 0, 0))

    table = {
        "w": row(width),
        "p": pl.BlockSpec((1, padded(seq_len), width), lambda g, t: (g + start, 0, 0)),
        "3w": row(3 * width),
        "l": row(LANES),
        "vec": pl.BlockSpec((8, width), lambda g, t: (0, 0)),
        "sum": pl.BlockSpec((1, 8, width), lambda g, t: (g + start, 0, 0)),
    }
    return [table[k] for k in kinds]


def attention_forward(tokens, gathered, vec, head_size, start, count):
    _, seq_len, width = tokens.shape
    table, sources = gathered
    specs = functools.partial(attention_specs, seq_len, width)
    shape = lambda c, t: jax.ShapeDtypeStruct((count, seq_len, c), t)
    return pl.pallas_call(
        functools.partial(forward_kernel, head_size, len(sources)),
        grid_spec=pltpu.PrefetchScalarGridSpec(
            num_scalar_prefetch=1,
            grid=(count,),
            in_specs=specs(start, ["w", "vec"]) + [ANY] * len(sources),
            out_specs=specs(0, ["w", "3w", "w", "w", "l", "p"]),
            scratch_shapes=[
                pltpu.VMEM((width, 4 * width), BF),
                pltpu.SemaphoreType.DMA((table.shape[0],)),
            ],
        ),
        out_shape=[
            shape(width, BF),
            shape(3 * width, BF),
            shape(width, BF),
            shape(width, F32),
            shape(LANES, F32),
            jax.ShapeDtypeStruct((count, padded(seq_len), width), BF),
        ],
        compiler_params=params(48),
        cost_estimate=cost(
            count * seq_len * width * (8 * width + 4 * seq_len),
            count * seq_len * width * 16 + 8 * width * width,
        ),
        name="attention_forward",
    )(table, tokens, vec, *sources)


def attention_backward(tokens, saved, dhid, cot, gathered, vec, head_size, start, count):
    _, seq_len, width = tokens.shape
    _, qkv, _, mid, lse, _ = saved
    table, sources = gathered
    specs = functools.partial(attention_specs, seq_len, width)
    shape = lambda c, t: jax.ShapeDtypeStruct((count, seq_len, c), t)
    in_specs = specs(start, ["w"]) + specs(0, ["3w", "w", "l"]) + specs(start, ["p"] * 4)
    in_specs = in_specs + specs(0, ["vec"]) + [ANY] * len(sources)
    return pl.pallas_call(
        functools.partial(backward_kernel, head_size, len(sources)),
        grid_spec=pltpu.PrefetchScalarGridSpec(
            num_scalar_prefetch=1,
            grid=(count,),
            in_specs=in_specs,
            out_specs=specs(0, ["3w", "w", "w", "sum"]),
            scratch_shapes=[
                pltpu.VMEM((seq_len, width), BF),
                pltpu.VMEM((width, 4 * width), BF),
                pltpu.SemaphoreType.DMA((table.shape[0],)),
            ],
        ),
        out_shape=[
            shape(3 * width, BF),
            shape(width, BF),
            shape(width, BF),
            jax.ShapeDtypeStruct((count, 8, width), F32),
        ],
        compiler_params=params(48),
        cost_estimate=cost(
            count * seq_len * width * (8 * width + 10 * seq_len),
            count * seq_len * width * 22 + 8 * width * width,
        ),
        name="attention_backward",
    )(table, tokens, qkv, mid, lse, *dhid, cot, vec, *sources)


def dense_grads_kernel(shards, team, parts, table, *refs):
    count = parts[1]
    lists = [refs[i * parts[0] : (i + 1) * parts[0]] for i in range(5)]
    rest = refs[5 * parts[0] :]
    extra = rest[: 1 + 2 * GROUPS]
    mine, other, small, weights, flat, piece = rest[1 + 2 * GROUPS :]
    width = weights.shape[0]
    here = width // shards
    quarter = here // team
    step = pl.program_id(0)

    for p in range(parts[0]):
        first, dproj, att, dbranch, _ = (each[p] for each in lists)

        @pl.when(step // count == p)
        def _(first=first, dproj=dproj, att=att, dbranch=dbranch, p=p):
            left = dot_tn(first[0], dproj[0])
            right = dot_tn(att[0], dbranch[0])
            if p:
                weights[:, : 3 * width] += left
                weights[:, 3 * width :] += right
            else:

                @pl.when(step == 0)
                def _():
                    weights[:, : 3 * width] = left
                    weights[:, 3 * width :] = right

                @pl.when(step > 0)
                def _():
                    weights[:, : 3 * width] += left
                    weights[:, 3 * width :] += right

    @pl.when(step == parts[0] * count - 1)
    def _():
        member = table[shards]
        half = team // 2
        for m in range(shards):
            base = table[m] * here
            for target, flip in ((mine, 0), (other, 1)):
                if team == 1 and flip:
                    continue
                for y in range(max(1, half)):
                    core = (member % 2) ^ flip if team > 1 else 0
                    row = core * (here // 2) if team > 1 else 0
                    if half > 1:
                        row = row + ((member // 2) ^ y) * quarter
                    at = pl.multiple_of(base + row, quarter)
                    target[y, m] = weights[pl.ds(at, quarter), :].astype(BF)
        total = jnp.zeros((8, width), F32)
        for sums in lists[4]:
            for i in range(count):
                total = total + sums[i]
        grt = extra[0][0:8, :]
        gdb = jnp.concatenate([extra[1 + g][...] for g in range(GROUPS)], axis=0)
        flat[...] = jnp.zeros_like(flat)
        flat[0:EXPERTS, :] = grt
        flat[SMALL_DOWN : SMALL_DOWN + EXPERTS, :] = gdb
        flat[SMALL_QV : SMALL_QV + 2, :] = total[3:5, :]
        flat[SMALL_VEC : SMALL_VEC + 2, :] = total[5:7, :]
        flat[SMALL_VEC + 2 : SMALL_VEC + 5, :] = total[0:3, :]
        low = flat[...].astype(BF)
        ups = [extra[1 + GROUPS + g][...] for g in range(GROUPS)]
        ring_low = jnp.concatenate(ups, axis=0).astype(BF)
        for m in range(shards):
            piece[...] = dot_nt(low, one_hot(here, width, table[m] * here))
            j = (shards - m) % shards
            at = pl.multiple_of(SMALL_UP + member * EXPERTS, 8)
            piece[pl.ds(at, EXPERTS), :] = dot_nt(ring_low, one_hot(here, width, j * here))
            small[m] = piece[...].astype(BF)


def dense_grads(links, firsts, dprojs, atts, dbranches, sums, grts, gdbs, gubs, rows):
    shards, team = links.shards, links.team
    parts = len(firsts)
    count, seq_len, width = firsts[0].shape
    here = width // shards
    quarter = here // team
    halves = max(1, team // 2)
    member = (links.my_copy() % team).astype(jnp.int32).reshape(1)
    table = jnp.concatenate([links.ahead_of(), member])

    def part(p, columns):
        return pl.BlockSpec(
            (1, seq_len, columns), lambda g, t: (jnp.clip(g - p * count, 0, count - 1), 0, 0)
        )

    whole = lambda a: pl.BlockSpec(a.shape, lambda g, t: (0,) * a.ndim)
    both = jax.ShapeDtypeStruct((halves, shards, quarter, 4 * width), BF)
    shapes = [both, both, jax.ShapeDtypeStruct((shards, rows, here), BF)]
    return pl.pallas_call(
        functools.partial(dense_grads_kernel, shards, team, (parts, count)),
        grid_spec=pltpu.PrefetchScalarGridSpec(
            num_scalar_prefetch=1,
            grid=(parts * count,),
            in_specs=[
                *[part(p, width) for p in range(parts)],
                *[part(p, 3 * width) for p in range(parts)],
                *[part(p, width) for p in range(parts)],
                *[part(p, width) for p in range(parts)],
                *[whole(a) for a in [*sums, *grts, *gdbs, *gubs]],
            ],
            out_specs=[whole(a) for a in shapes],
            scratch_shapes=[
                pltpu.VMEM((width, 4 * width), F32),
                pltpu.VMEM((rows, width), F32),
                pltpu.VMEM((rows, here), F32),
            ],
        ),
        out_shape=shapes,
        compiler_params=params(48),
        cost_estimate=cost(8 * parts * count * seq_len * width * width, 12 * width * width),
        name="dense_grads",
    )(table, *firsts, *dprojs, *atts, *dbranches, *sums, *grts, *gdbs, *gubs)


class Steps:
    def __init__(self, chain):
        self.chain, self.result, self.flying = chain, None, None
        self.advance(None)

    def advance(self, arrived):
        try:
            self.flying = self.chain.send(arrived)
        except StopIteration as end:
            self.flying, self.result = None, end.value

    def finish(self):
        while self.flying is not None:
            self.advance(self.flying)
        return self.result


def stage(chains, work):
    flying, work = lax.optimization_barrier(([c.flying for c in chains], work))
    for chain, arrived in zip(chains, flying):
        if arrived is not None:
            chain.advance(arrived)
    return work


def gather_team(links, value):
    blocks = [value]
    for bit in reversed(links.team_bits):
        arrived = yield [links.swap(b, bit) for b in blocks]
        blocks = blocks + arrived
    return blocks


def reduce_team(links, keep, give):
    if links.team == 1:
        return keep, jnp.zeros_like(keep), jnp.zeros_like(keep)
    other = yield links.swap(give, 1)
    if links.team == 2:
        return keep, other, jnp.zeros_like(keep)
    half = keep.shape[0] // 2
    far = yield links.swap(add_low(keep[half:], other[half:]), 2)
    return keep, other, far


def ring_gather_dense(links, mine, other, small):
    count = links.shards
    mines, others, smalls = [mine], [other], [small]
    mines += [None] * (count - 1)
    others += [None] * (count - 1)
    smalls += [None] * (count - 1)
    forward = backward = (mine, small)
    fresh = []
    for j in range(1, count // 2 + 2):
        ring = ()
        if j <= count // 2:
            ring = (tuple(links.ring_ahead(v) for v in forward),)
            if count - j > j:
                ring += (tuple(links.ring_back(v) for v in backward),)
        swaps = [links.swap(mines[k], 1) for k in fresh] if links.halves > 1 else []
        ring, swaps = yield (ring, swaps)
        for k, v in zip(fresh, swaps):
            others[k] = v
        fresh = []
        if ring:
            forward = ring[0]
            mines[j], smalls[j] = forward
            fresh.append(j)
        if len(ring) > 1:
            backward = ring[1]
            mines[count - j], smalls[count - j] = backward
            fresh.append(count - j)
    return mines, others, smalls


def ring_gather_pair(links, value):
    half = links.shards // 2
    near, far = [value], []
    forward = backward = value
    for _ in range(1, half):
        forward, backward = yield (links.ring_ahead(forward), links.ring_back(backward))
        near.append(forward)
        far.append(backward)
    halves = yield (links.ring_ahead(forward[0]), links.ring_back(backward[1]))
    return near + list(halves) + far[::-1]


def ring_reduce_pair(links, value):
    count = links.shards
    half = count // 2
    up, down = yield (links.ring_back(value[half, 0]), links.ring_ahead(value[half, 1]))
    back = jnp.stack([add_low(value[half - 1, 0], up), value[half - 1, 1]])
    ahead = jnp.stack([value[half + 1, 0], add_low(value[half + 1, 1], down)])
    for j in range(half - 2, -1, -1):
        back, ahead = yield (links.ring_back(back), links.ring_ahead(ahead))
        if j:
            back = add_low(value[j], back)
            ahead = add_low(value[count - j], ahead)
    total = (value[0].astype(F32) + back.astype(F32) + ahead.astype(F32)).astype(BF)
    for bit in links.other_bits:
        other = yield links.swap(total, bit)
        total = add_low(total, other)
    return total


def reduce_dense(links, mine, other, small):
    count = links.shards
    half = count // 2
    value = mine
    if links.team > 1:
        swapped, small_swapped = yield (links.swap(other, 1), links.swap(small, 1))
        value = add_low(mine, swapped)
        small = add_low(small, small_swapped)
    if links.team > 2:
        swapped, small_swapped = yield (links.swap(value[1], 2), links.swap(small, 2))
        value = add_low(value[0], swapped)
        small = add_low(small, small_swapped)
    else:
        value = value[0]
    values = [value, small]
    totals = [v[0].astype(F32) for v in values]
    ahead = [v[half] for v in values]
    back = [v[half + 1] for v in values]
    for m in range(half - 1, -1, -1):
        n = count - m
        flying = ([links.ring_ahead(a) for a in ahead], [])
        if n - 1 > half:
            flying = (flying[0], [links.ring_back(b) for b in back])
        ahead, arrived = yield flying
        if arrived:
            back = arrived
            if n < count:
                back = [add_low(b, v[n]) for b, v in zip(back, values)]
        if m:
            ahead = [add_low(a, v[m]) for a, v in zip(ahead, values)]
    total, small = [
        t + a.astype(F32) + b.astype(F32) for t, a, b in zip(totals, ahead, back)
    ]
    for bit in links.other_bits:
        other_total, other_small = yield (links.swap(total, bit), links.swap(small, bit))
        total, small = total + other_total, small + other_small
    value = total.astype(BF)
    for bit in reversed(links.team_bits):
        swapped = yield links.swap(value, bit)
        upper = (links.my_copy() & bit) != 0
        value = jnp.concatenate(
            [jnp.where(upper, swapped, value), jnp.where(upper, value, swapped)], axis=0
        )
    return value.astype(F32), small


def local(
    links,
    tokens,
    routes,
    live_images,
    cotangent,
    norm_one_gain,
    norm_one_bias,
    qkv_weight,
    query_value_bias,
    output_weight,
    output_bias,
    norm_two_gain,
    norm_two_bias,
    router_weight,
    expert_up,
    expert_up_bias,
    expert_down,
    expert_down_bias,
):
    shards = links.shards
    images_here, seq_len, width = tokens.shape
    head_size = width // HEADS
    d_rows = qkv_weight.shape[0]
    ff_rows = expert_down.shape[1]
    size = EXPERTS // GROUPS

    mine, other, small = pack_dense(
        links,
        (
            qkv_weight,
            output_weight,
            router_weight,
            query_value_bias,
            norm_one_gain,
            norm_one_bias,
            norm_two_gain,
            norm_two_bias,
            output_bias,
            expert_down_bias,
            expert_up_bias,
        ),
    )
    mine, other, small, up_arg, down_arg, cotangent, routes = lax.optimization_barrier(
        (mine, other, small, expert_up, expert_down, cotangent, routes)
    )
    dense = Steps(ring_gather_dense(links, mine, other, small))
    packed = pack_experts(links, up_arg, down_arg, 0, EXPERTS)
    packed = stage([dense], packed)
    kept = keep_live(live_images, cotangent)
    route_chain = Steps(gather_team(links, jnp.swapaxes(routes, 1, 2)))
    kept, packed = stage([dense, route_chain], (kept, packed))
    packed = stage([dense, route_chain], packed)
    ring = Steps(ring_gather_pair(links, packed))
    positions, meta = route_tables(route_chain.finish(), EXPERTS)
    positions, meta = stage([dense], (positions, meta))
    dense.finish()
    mines, others, smalls = dense.result
    sources, offsets = mines, links.behind() * d_rows
    if links.halves > 1:
        core = links.my_copy() % 2
        half_rows = d_rows // 2
        offsets = jnp.concatenate(
            [offsets + core * half_rows, offsets + (1 - core) * half_rows]
        )
        sources = mines + others
    sources, smalls, kept = lax.optimization_barrier((sources, smalls, kept))
    gathered = (offsets.astype(jnp.int32), sources)

    cots = Steps(gather_team(links, kept))
    vec, router_rows, down_bias, up_ring = unpack_small(links, smalls)
    saved = attention_forward(tokens, gathered, vec, head_size, 0, images_here)
    saved, router_rows = stage([ring, cots], (saved, router_rows))
    hid_chain = Steps(gather_team(links, saved[5]))
    stage([ring, cots, hid_chain], ())
    cots.finish()
    hids = [hid_chain.finish()]
    *rows, probs = dispatch(hids, cots.result, positions, meta, router_rows)
    rows, probs, hids = stage([ring], (rows, probs, hids))
    weights = ring.finish()

    outs = [expert_call(links, rows, weights, up_ring, down_bias, meta, 0, size)]
    outs[0] = stage([], outs[0])
    reduces = [Steps(ring_reduce_pair(links, outs[0][3]))]
    rows = lax.optimization_barrier((rows, outs[0][4]))[0]
    outs.append(expert_call(links, rows, weights, up_ring, down_bias, meta, 1, size))
    outs[1] = stage(reduces, outs[1])
    reduces.append(Steps(ring_reduce_pair(links, outs[1][3])))
    mix_keep, mix_give, dhid_keep, dhid_give, grt = stage(
        reduces, combine([o[:3] for o in outs], hids, positions, probs, router_rows, meta, size)
    )
    dhidden = Steps(reduce_team(links, dhid_keep, dhid_give)).finish()
    dhidden = stage(reduces, dhidden)

    mixtures = Steps(reduce_team(links, *lax.optimization_barrier((mix_keep, mix_give, dhidden))[:2]))
    dproj, dbranch, grad_tokens, sums = attention_backward(
        tokens, saved, dhidden, kept, gathered, vec, head_size, 0, images_here
    )
    mine, other, small_parts = dense_grads(
        links,
        [saved[0]],
        [dproj],
        [saved[2]],
        [dbranch],
        [sums],
        [grt],
        [o[5] for o in outs],
        [o[4] for o in outs],
        small.shape[0],
    )
    mixture = mixtures.finish()
    mine, other, small_parts, mixture, grad_tokens = stage(
        reduces, (mine, other, small_parts, mixture, grad_tokens)
    )
    mixed = finish_mixed(live_images, saved[3], mixture)

    last = Steps(reduce_dense(links, mine, other, small_parts))
    first_half = Steps(gather_team(links, reduces[0].finish()))
    mixed, grad_tokens = stage([reduces[1], last, first_half], (mixed, grad_tokens))
    second_half = Steps(gather_team(links, reduces[1].finish()))
    stage([last, first_half, second_half], ())
    placed = place_experts(links, first_half.finish(), 0, ())
    placed = place_experts(links, second_half.finish(), size, placed)
    total, share = last.finish()
    vector = [share[SMALL_VEC + i] for i in range(5)]
    up_rows = share[SMALL_UP:].reshape(ff_rows // d_rows, EXPERTS, d_rows)
    grad_up_bias = jnp.swapaxes(up_rows, 0, 1).reshape(EXPERTS, ff_rows)
    return (
        mixed,
        grad_tokens,
        vector[0],
        vector[1],
        total[:, : 3 * width],
        share[SMALL_QV : SMALL_QV + 2],
        total[:, 3 * width :],
        vector[4],
        vector[2],
        vector[3],
        share[:EXPERTS].T,
        placed[0],
        grad_up_bias,
        placed[1],
        share[SMALL_DOWN : SMALL_DOWN + EXPERTS],
    )


def solution(mesh):
    links = Links(mesh.shape["shard"], mesh.shape["replica"])
    both = ("shard", "replica")
    return jax.shard_map(
        functools.partial(local, links),
        mesh=mesh,
        in_specs=(
            P(both, None, None),
            P(both, None, None),
            P(both),
            P(both, None, None),
            P("shard"),
            P("shard"),
            P("shard", None),
            P(None, "shard"),
            P("shard", None),
            P("shard"),
            P("shard"),
            P("shard"),
            P("shard", None),
            P(None, None, "shard"),
            P(None, "shard"),
            P(None, "shard", None),
            P(None, "shard"),
        ),
        out_specs=(
            P(both, None, None),
            P(both, None, None),
            P("shard"),
            P("shard"),
            P("shard", None),
            P(None, "shard"),
            P("shard", None),
            P("shard"),
            P("shard"),
            P("shard"),
            P("shard", None),
            P(None, None, "shard"),
            P(None, "shard"),
            P(None, "shard", None),
            P(None, "shard"),
        ),
        check_vma=False,
    )
```
